512 devices in a mesh: line: 128 (over z, x, core), tm: 4 (over y).
Axes of the slice: x: 4, y: 4, z: 16, core: 2. Of those that a mesh axis runs over, the one named last changes fastest.
Arguments:
- traces: float32 [128, 512, 4, 512], P('line', None, None, 'tm'), may hold values from -40 to 40
- rates: int32 [128, 4, 8, 32], P('line', 'tm'), may hold values from 16 to 188
- byte_target: int32 [1], replicated, may hold values from 160 to 319
Outputs:
- coefficients: float32 [32, 2048, 4, 512], P(None, 'line', None, 'tm')
The draws below stay inside these ranges and needn't reach their ends.
All inputs are finite; a program needn't handle non-finite values.
Results may differ from the reference program's by a relative error of at most 0.0003.
Values sent between devices are 32-bit elements; how exact they have to be, the bound alone decides.
A program may use at most 64 MiB of HBM per device.

```python
import math
import jax
import jax.numpy as jnp
from jax import lax

REC_DEV = 16
NT = 2048
PLANES = 8
BISECT = 12
SHOTS = 32
LINES = 128
BANDS = 4
RECV = 2048
TBLK = 512
TB_DEV = 128


def draw_traces(key, part):
    key = jax.random.fold_in(key, 11)
    key_noise, key_receiver, key_time = jax.random.split(key, 3)
    receiver_axis = jnp.arange(RECV, dtype=jnp.float32) / RECV
    receiver_rough = jnp.exp(jax.random.uniform(key_receiver, (RECV,), jnp.float32, math.log(0.6), math.log(1.6)))
    receiver_gain = (0.6 + 1.2 * receiver_axis) * receiver_rough
    sample_time = (4.0 * jnp.arange(TBLK, dtype=jnp.float32)[None, :] + jnp.arange(4, dtype=jnp.float32)[:, None]) / NT
    time_rough = jnp.exp(jax.random.uniform(key_time, (4, TBLK), jnp.float32, math.log(0.7), math.log(1.4)))
    time_gain = (0.35 + 2.0 * jnp.exp(-3.0 * sample_time)) * time_rough
    full_shape = (SHOTS, RECV, 4, TBLK)
    source = jnp.clip(jax.random.normal(key_noise, full_shape, jnp.float32), -4.0, 4.0)
    values = jnp.clip(source * receiver_gain[None, :, None, None] * time_gain[None, None, :, :], -40.0, 40.0)
    values = values.reshape(SHOTS, LINES, 4, REC_DEV // 4, 4, TBLK)
    return jnp.transpose(values, (0, 2, 1, 3, 4, 5)).reshape(4 * SHOTS, RECV // 4, 4, TBLK)


def draw_rates(key, part):
    key = jax.random.fold_in(key, 23)
    base_rate = jax.random.randint(key, (LINES, BANDS, PLANES, SHOTS), 16, 64, dtype=jnp.int32)
    base_rate = base_rate.at[LINES - 1, 0, 0, 0].set(63).at[0, 0, 0, 0].set(16)
    line_index = jnp.arange(LINES, dtype=jnp.int32)[:, None, None, None]
    return base_rate * (LINES + 2 * line_index) // LINES


def setup_inputs(seed: int = 0) -> dict:
    seeds = jax.random.split(jax.random.key(seed), 4)
    traces = draw_traces(jax.random.fold_in(seeds[3], 71), 0)
    rates = draw_rates(jax.random.fold_in(seeds[3], 71), 0)
    byte_target = jax.random.randint(seeds[2], (1,), 20 * PLANES, 40 * PLANES).astype(jnp.int32)
    return dict(traces=traces, rates=rates, byte_target=byte_target)


slope_floor = -12.0
slope_span = 32.0
rate_scale = 65536.0

def detail(even_part, odd_part, ahead_even):
    return odd_part - 0.5 * (even_part + ahead_even)

def smooth(even_part, behind, details):
    return even_part + 0.25 * (behind + details)

def next_along(values):
    return jnp.concatenate([values[..., 1:], jnp.zeros_like(values[..., :1])], axis=-1)

def prior_along(values):
    return jnp.concatenate([jnp.zeros_like(values[..., :1]), values[..., :-1]], axis=-1)

def time_first(signal):
    phase_zero, phase_one, phase_two, phase_three = (signal[:, 0], signal[:, 1], signal[:, 2], signal[:, 3])
    detail_one = detail(phase_zero, phase_one, phase_two)
    detail_three = detail(phase_two, phase_three, next_along(phase_zero))
    smooth_zero = smooth(phase_zero, prior_along(detail_three), detail_one)
    smooth_two = smooth(phase_two, detail_one, detail_three)
    return jnp.stack([smooth_zero, detail_one, smooth_two, detail_three], axis=1)

def time_pair(even_part, odd_part):
    details = detail(even_part, odd_part, next_along(even_part))
    return (smooth(even_part, prior_along(details), details), details)

def receiver_lift(series):
    even_part = series[0::2]
    odd_part = series[1::2]
    ahead_even = jnp.concatenate([even_part[1:], jnp.zeros_like(even_part[:1])], axis=0)
    details = detail(even_part, odd_part, ahead_even)
    behind = jnp.concatenate([jnp.zeros_like(details[:1]), details[:-1]], axis=0)
    lowpass = smooth(even_part, behind, details)
    return jnp.stack([lowpass, details], axis=1).reshape(series.shape)

def transform(signal):
    lifted = receiver_lift(time_first(signal))
    rows_even = lifted[0::2]
    rows_odd = lifted[1::2]
    lowpass, details = time_pair(rows_even[:, 0], rows_even[:, 2])
    band_two = receiver_lift(jnp.stack([lowpass, details], axis=1))
    even_new = jnp.stack([band_two[:, 0], rows_even[:, 1], band_two[:, 1], rows_even[:, 3]], axis=1)
    return jnp.stack([even_new, rows_odd], axis=1).reshape(lifted.shape)

def plane_gains(coeffs):
    blocks = coeffs.reshape(LINES, REC_DEV, 4, BANDS, TB_DEV)
    square = blocks * blocks
    planes_out = []
    for plane_index in range(PLANES):
        bottom_sq = 4.0 ** (3 - plane_index)
        top_sq = 4.0 ** (4 - plane_index)
        planes_out.append(lax.optimization_barrier(jnp.sum(jnp.clip(square, bottom_sq, top_sq) - bottom_sq, axis=(1, 2, 4))))
    return jnp.stack(planes_out)

def slope_at(grid_index):
    return jnp.exp2(slope_floor + grid_index.astype(jnp.float32) * (slope_span / 2 ** BISECT))

def reference(traces, rates, byte_target):
    ordered = traces.reshape(SHOTS, 4, LINES, REC_DEV // 4, 4, TBLK)
    ordered = jnp.transpose(ordered, (0, 2, 1, 3, 4, 5)).reshape(SHOTS, RECV, 4, TBLK)

    def per_shot(signal):
        coeffs = transform(signal)
        return (coeffs, plane_gains(coeffs))
    wavelet, plane_gain = lax.map(per_shot, ordered)
    rate_table = jnp.transpose(rates, (3, 2, 0, 1))
    rate_float = rate_table.astype(jnp.float32)
    byte_limit = byte_target[0] * (SHOTS * LINES * BANDS)

    def kept(grid_index):
        chosen_rates = jnp.where(plane_gain >= slope_at(grid_index) * rate_float, rate_table, 0)
        return jnp.sum(chosen_rates, dtype=jnp.int32)
    bottom = jnp.int32(0)
    ceiling = jnp.int32(2 ** BISECT)
    for bisect_turn in range(BISECT):
        middle = (bottom + ceiling) // 2
        within = kept(middle) <= byte_limit
        ceiling = jnp.where(within, middle, ceiling)
        bottom = jnp.where(within, bottom, middle)
    slope_now = slope_at(ceiling)
    totals = lax.optimization_barrier(jnp.sum(rate_table, axis=1)).astype(jnp.float32)
    shrink_by = jnp.sqrt(slope_now * totals / rate_scale)

    def shrink(pair_args):
        coeffs, limits = pair_args
        spread_limits = jnp.repeat(jnp.repeat(limits, REC_DEV, axis=0), TB_DEV, axis=1)[:, None, :]
        return coeffs - jnp.clip(coeffs, -spread_limits, spread_limits)
    return lax.map(shrink, (wavelet, shrink_by))
```

```python
import jax
import jax.numpy as jnp
from jax import lax
from jax.experimental import pallas as pl
from jax.experimental.pallas import tpu as pltpu
from jax.sharding import PartitionSpec as P

PLANES = 8
BISECT = 12
MESH = pl.DeviceIdType.MESH

slope_floor = -12.0
slope_span = 32.0
rate_scale = 65536.0


def shifted(value, axis, steps):
    count = lax.axis_size(axis)
    initial, last = (max(0, -steps), min(count, count - steps))
    return lax.ppermute(value, axis, [(source, source + steps) for source in range(initial, last)])


def detail(even_part, odd_part, ahead_even):
    return odd_part - 0.5 * (even_part + ahead_even)


def smooth(even_part, behind, details):
    return even_part + 0.25 * (behind + details)


def time_ahead(values):
    return shifted(values, "tm", -1)


def time_behind(values):
    return shifted(values, "tm", 1)


def line_ahead(values):
    return shifted(values, "line", -1)


def line_behind(values):
    return shifted(values, "line", 1)


def time_first(signal):
    phase_zero, phase_one, phase_two, phase_three = (
        signal[:, :, 0],
        signal[:, :, 1],
        signal[:, :, 2],
        signal[:, :, 3],
    )
    ahead_even = jnp.concatenate([phase_zero[:, :, 1:], time_ahead(phase_zero[:, :, :1])], axis=2)
    detail_one = detail(phase_zero, phase_one, phase_two)
    detail_three = detail(phase_two, phase_three, ahead_even)
    behind = jnp.concatenate(
        [time_behind(detail_three[:, :, -1:]), detail_three[:, :, :-1]], axis=2
    )
    smooth_zero = smooth(phase_zero, behind, detail_one)
    smooth_two = smooth(phase_two, detail_one, detail_three)
    return jnp.stack([smooth_zero, detail_one, smooth_two, detail_three], axis=2)


def time_pair(even_part, odd_part):
    ahead_even = jnp.concatenate([even_part[:, :, 1:], time_ahead(even_part[:, :, :1])], axis=2)
    details = detail(even_part, odd_part, ahead_even)
    behind = jnp.concatenate([time_behind(details[:, :, -1:]), details[:, :, :-1]], axis=2)
    return (smooth(even_part, behind, details), details)


def line_rims(even_part, odd_part):
    ahead_even = jnp.concatenate([even_part[:, 1:], line_ahead(even_part[:, :1])], axis=1)
    details = detail(even_part, odd_part, ahead_even)
    behind = jnp.concatenate([line_behind(details[:, -1:]), details[:, :-1]], axis=1)
    return (details, behind)


def receiver_lift(series):
    even_part = series[:, 0::2]
    odd_part = series[:, 1::2]
    details, behind = line_rims(even_part, odd_part)
    lowpass = smooth(even_part, behind, details)
    return jnp.stack([lowpass, details], axis=2).reshape(series.shape)


def finish(signal):
    lifted = receiver_lift(signal)
    rows_even = lifted[:, 0::2]
    rows_odd = lifted[:, 1::2]
    lowpass, details = time_pair(rows_even[:, :, 0], rows_even[:, :, 2])
    band_two = receiver_lift(jnp.stack([lowpass, details], axis=2))
    even_new = jnp.stack(
        [band_two[:, :, 0], rows_even[:, :, 1], band_two[:, :, 1], rows_even[:, :, 3]], axis=2
    )
    return jnp.stack([even_new, rows_odd], axis=2).reshape(lifted.shape)


def slope_at(grid_index):
    return jnp.exp2(slope_floor + grid_index.astype(jnp.float32) * (slope_span / 2**BISECT))


def regroup_kernel(x_ref, o_ref, ssem, rsem, lsem):
    n = 128
    me = lax.axis_index("line")
    bar = pltpu.get_barrier_semaphore()

    @pl.loop(0, n - 1)
    def _(i):
        pl.semaphore_signal(
            bar, inc=1, device_id={"line": lax.rem(me + i + 1, n)}, device_id_type=MESH
        )

    pl.semaphore_wait(bar, n - 1)
    mine = o_ref.at[pl.ds(pl.multiple_of(me * 16, 16), 16)]

    @pl.loop(0, n - 1)
    def _(i):
        target = lax.rem(me + i + 1, n)
        pltpu.make_async_remote_copy(
            src_ref=x_ref.at[pl.ds(pl.multiple_of(target * 16, 16), 16)],
            dst_ref=mine,
            send_sem=ssem,
            recv_sem=rsem,
            device_id={"line": target},
            device_id_type=MESH,
        ).start()

    own = pltpu.make_async_copy(x_ref.at[pl.ds(pl.multiple_of(me * 16, 16), 16)], mine, lsem)
    own.start()
    own.wait()
    most = o_ref.at[pl.ds(0, (n - 1) * 16)]
    pltpu.make_async_copy(most, most, rsem).wait()
    pltpu.make_async_copy(most, most, ssem).wait()


def regroup(rows):
    return pl.pallas_call(
        regroup_kernel,
        out_shape=jax.ShapeDtypeStruct(rows.shape, rows.dtype),
        in_specs=[pl.BlockSpec(memory_space=pl.ANY)],
        out_specs=pl.BlockSpec(memory_space=pl.ANY),
        scratch_shapes=[pltpu.SemaphoreType.DMA] * 3,
        compiler_params=pltpu.CompilerParams(collective_id=1, has_side_effects=True),
        name="regroup",
    )(rows)


def body(traces, rates, byte_target):
    line_count = lax.axis_size("line")
    band_count = lax.axis_size("tm")
    width = traces.shape[3]
    gathered = regroup(traces.reshape(2048, width)).reshape(32, 16, 4, width)
    wavelet = finish(time_first(gathered))
    square = wavelet * wavelet
    planes_out = []
    for plane_index in range(PLANES):
        bottom_sq = 4.0 ** (3 - plane_index)
        top_sq = 4.0 ** (4 - plane_index)
        planes_out.append(jnp.sum(jnp.clip(square, bottom_sq, top_sq) - bottom_sq, axis=(1, 2, 3)))
    plane_gain = jnp.stack(planes_out)
    rate_table = rates.reshape(rates.shape[2], rates.shape[3])
    rate_float = rate_table.astype(jnp.float32)
    byte_limit = byte_target[0] * (wavelet.shape[0] * line_count * band_count)

    trials = slope_at(jnp.arange(2**BISECT, dtype=jnp.int32))[:, None, None]
    kept = jnp.sum(
        jnp.where(plane_gain[None] >= trials * rate_float[None], rate_table[None], 0),
        axis=(1, 2),
        dtype=jnp.int32,
    )
    kept = lax.psum(kept, ("line", "tm"))
    chosen = 1 + jnp.sum((kept[1:] > byte_limit).astype(jnp.int32))
    slope_now = slope_at(chosen)
    rate_sums = jnp.sum(rate_table, axis=0).astype(jnp.float32)
    shrink_by = jnp.sqrt(slope_now * rate_sums / rate_scale)[:, None, None, None]
    return wavelet - jnp.clip(wavelet, -shrink_by, shrink_by)


def solution(mesh):
    return jax.shard_map(
        body,
        mesh=mesh,
        in_specs=(P("line", None, None, "tm"), P("line", "tm", None, None), P()),
        out_specs=P(None, "line", None, "tm"),
        check_vma=False,
    )
```

```python
import jax
import jax.numpy as jnp
from jax import lax
from jax.experimental import pallas as pl
from jax.experimental.pallas import tpu as pltpu
from jax.sharding import PartitionSpec as P

PLANES = 8
BISECT = 12
LINES = 128
BANDS = 4
SHOTS = 32
GROUPS = 4
ROWS = 2048
SLOPE_ROWS = 2**BISECT // 128
MESH = pl.DeviceIdType.MESH

slope_floor = -12.0
slope_span = 32.0
rate_scale = 65536.0

PLANE_STEPS = sorted(
    [(dx, dc, dy) for dx in range(4) for dc in range(2) for dy in range(4)][1:],
    key=lambda s: (-(min(s[0], 4 - s[0]) + min(s[2], 4 - s[2])), s),
)
RING_STEPS = sorted(range(1, 16), key=lambda s: -min(s, 16 - s))


def remote(src, dst, ssem, rsem, line, tm):
    return pltpu.make_async_remote_copy(
        src_ref=src,
        dst_ref=dst,
        send_sem=ssem,
        recv_sem=rsem,
        device_id=(line, tm),
        device_id_type=MESH,
    )


def settle(ref, sem):
    pltpu.make_async_copy(ref, ref, sem).wait()


def detail(even_part, odd_part, ahead_even):
    return odd_part - 0.5 * (even_part + ahead_even)


def smooth(even_part, behind, details):
    return even_part + 0.25 * (behind + details)


def kernel(
    x_ref,
    rates_ref,
    target_ref,
    w_ref,
    shrink_ref,
    held,
    lifted,
    wave,
    time_send,
    time_recv,
    ahead_send,
    ahead_recv,
    back_send,
    back_recv,
    slopes,
    rate_cols,
    kept_acc,
    kept_rows,
    plane_slots,
    ring_row,
    ring_slots,
    count_row,
    count_slots,
    all_sems,
    time_sems,
    line_sems,
    tree_sems,
):
    line = lax.axis_index("line")
    tm = lax.axis_index("tm")
    z = line // 8
    x = (line // 2) % 4
    core = line % 2

    def plane_peer(step):
        dx, dc, dy = step
        peer_x = lax.rem(x + dx, 4)
        peer_core = lax.rem(core + dc, 2)
        return z * 8 + peer_x * 2 + peer_core, lax.rem(tm + dy, 4)

    def plane_index(line_at, tm_at):
        return (line_at % 8) * 4 + tm_at

    bar = pltpu.get_barrier_semaphore()

    @pl.loop(0, LINES - 1)
    def _(i):
        pl.semaphore_signal(
            bar, inc=1, device_id=(lax.rem(line + i + 1, LINES), tm), device_id_type=MESH
        )

    others = [s for s in PLANE_STEPS if s[2]]
    for step in others:
        pl.semaphore_signal(bar, inc=1, device_id=plane_peer(step), device_id_type=MESH)
    pl.semaphore_wait(bar, LINES - 1 + len(others))

    mine = held.at[pl.ds(pl.multiple_of(line * 16, 16), 16)]

    @pl.loop(0, LINES - 1)
    def _(i):
        to = lax.rem(line + i + 1, LINES)
        remote(
            x_ref.at[pl.ds(pl.multiple_of(to * 16, 16), 16)],
            mine,
            all_sems.at[0],
            all_sems.at[1],
            to,
            tm,
        ).start()

    own = pltpu.make_async_copy(
        x_ref.at[pl.ds(pl.multiple_of(line * 16, 16), 16)], mine, all_sems.at[2]
    )
    own.start()

    lane = lax.broadcasted_iota(jnp.int32, (8, 128), 1)
    sub = lax.broadcasted_iota(jnp.int32, (8, 128), 0)
    for row in range(SLOPE_ROWS):
        grid_index = (lane + row * 128).astype(jnp.float32)
        slopes[row] = jnp.exp2(slope_floor + grid_index * (slope_span / 2**BISECT))
        kept_acc[row] = jnp.zeros((8, 128), jnp.float32)
    for group in range(GROUPS):
        total = jnp.zeros((8, 128), jnp.float32)
        for plane in range(PLANES):
            rate_row = rates_ref[plane : plane + 1, :].astype(jnp.float32)
            picked = jnp.where(
                lane[:, :SHOTS] == sub[:, :SHOTS] + group * 8,
                jnp.broadcast_to(rate_row, (8, SHOTS)),
                0.0,
            )
            column = jnp.broadcast_to(jnp.sum(picked, axis=1, keepdims=True), (8, 128))
            rate_cols[plane, group * 8 : group * 8 + 8] = column
            total = total + column
        rate_cols[PLANES, group * 8 : group * 8 + 8] = total

    own.wait()
    most = held.at[pl.ds(0, ROWS - 16)]
    settle(most, all_sems.at[1])

    def phases(group, r):
        return [held[pl.ds(group * 512 + r * 4 + q, 8, stride=64), :] for q in range(4)]

    def span(group):
        return pl.ds(pl.multiple_of(group * 8, 8), 8)

    up = lax.rem(tm + 1, 4)
    down = lax.rem(tm + 3, 4)

    def time_copy(way, group):
        to = up if way == 0 else down
        return remote(
            time_send.at[way, span(group)],
            time_recv.at[way, span(group)],
            time_sems.at[0, way, group],
            time_sems.at[1, way, group],
            line,
            to,
        )

    @pl.loop(0, GROUPS)
    def _(group):
        to_next = jnp.zeros((8, 128), jnp.float32)
        to_prev = jnp.zeros((8, 128), jnp.float32)
        for r in range(16):
            p0, p1, p2, p3 = phases(group, r)
            d1 = detail(p0, p1, p2)
            d3 = detail(p2, p3, pltpu.roll(p0, 127, 1))
            s0 = smooth(p0, pltpu.roll(d3, 1, 1), d1)
            rim_detail = p3 - 0.5 * p2
            rim_second = p2 + 0.25 * d1 - 0.5 * s0
            rim_smooth = p0 + 0.25 * d1
            at = 2 * r
            to_next = jnp.where(lane == at, pltpu.roll(rim_detail, at + 1, 1), to_next)
            to_next = jnp.where(lane == at + 1, pltpu.roll(rim_second, at + 2, 1), to_next)
            to_prev = jnp.where(lane == at, pltpu.roll(p0, at, 1) if at else p0, to_prev)
            to_prev = jnp.where(lane == at + 1, pltpu.roll(rim_smooth, at + 1, 1), to_prev)
        time_send[0, span(group)] = to_next
        time_send[1, span(group)] = to_prev
        time_copy(0, group).start()
        time_copy(1, group).start()

    has_prev_band = jnp.where(tm > 0, 1.0, 0.0)
    has_next_band = jnp.where(tm < BANDS - 1, 1.0, 0.0)
    has_prev_line = jnp.where(line > 0, 1.0, 0.0)
    has_next_line = jnp.where(line < LINES - 1, 1.0, 0.0)
    line_up = lax.rem(line + 1, LINES)
    line_down = lax.rem(line + LINES - 1, LINES)

    def line_copy(way, group):
        if way == 0:
            return remote(
                ahead_send.at[:, span(group)],
                ahead_recv.at[:, span(group)],
                line_sems.at[0, 0, group],
                line_sems.at[1, 0, group],
                line_down,
                tm,
            )
        return remote(
            back_send.at[:, span(group)],
            back_recv.at[:, span(group)],
            line_sems.at[0, 1, group],
            line_sems.at[1, 1, group],
            line_up,
            tm,
        )

    @pl.loop(0, GROUPS)
    def _(group):
        time_copy(0, group).wait_recv()
        time_copy(1, group).wait_recv()
        from_prev = time_recv[0, span(group)]
        from_next = time_recv[1, span(group)]
        low = []
        high = []
        one = []
        three = []
        for r in range(16):
            at = 2 * r
            p0, p1, p2, p3 = phases(group, r)
            d1 = detail(p0, p1, p2)
            ahead = jnp.where(
                lane == 127,
                pltpu.roll(from_next, 127 - at, 1) * has_next_band,
                pltpu.roll(p0, 127, 1),
            )
            d3 = detail(p2, p3, ahead)
            rim = pltpu.roll(from_prev, 128 - at, 1) if at else from_prev
            d3_prev = (rim - 0.5 * p0) * has_prev_band
            s0 = smooth(p0, jnp.where(lane == 0, d3_prev, pltpu.roll(d3, 1, 1)), d1)
            s2 = smooth(p2, d1, d3)
            next_s0 = (pltpu.roll(from_next, 126 - at, 1) + 0.25 * d3) * has_next_band
            second = detail(s0, s2, jnp.where(lane == 127, next_s0, pltpu.roll(s0, 127, 1)))
            rim = pltpu.roll(from_prev, 127 - at, 1)
            second_prev = (rim + 0.25 * d3_prev - 0.5 * s0) * has_prev_band
            first = smooth(
                s0, jnp.where(lane == 0, second_prev, pltpu.roll(second, 1, 1)), second
            )
            for slot, value in enumerate((s0, d1, s2, d3, first, second)):
                lifted[slot, r, span(group)] = value
            if r == 0:
                for slot, value in enumerate((s0, d1, s2, d3, first, second)):
                    ahead_send[slot, span(group)] = value
            one.append(d1)
            three.append(d3)
            low.append(first)
            high.append(second)
        for slot, value in enumerate((low, high)):
            ahead_send[6 + slot, span(group)] = value[0] + 0.25 * detail(value[0], value[1], value[2])
            d5 = detail(value[10], value[11], value[12])
            d6 = detail(value[12], value[13], value[14])
            s6 = smooth(value[12], d5, d6)
            back_send[4 + slot, span(group)] = value[14] + 0.25 * d6 - 0.5 * s6
        for slot, value in enumerate((one, three, low, high)):
            back_send[slot, span(group)] = value[15] - 0.5 * value[14]
        line_copy(0, group).start()
        line_copy(1, group).start()

    @pl.loop(0, GROUPS)
    def _(group):
        line_copy(0, group).wait_recv()
        line_copy(1, group).wait_recv()
        gains = [jnp.zeros((8, 128), jnp.float32) for _ in range(PLANES)]

        def put(r, q, value):
            wave[pl.ds(group * 512 + r * 4 + q, 8, stride=64), :] = value
            square = value * value
            capped = [jnp.minimum(square, 4.0 ** (4 - p)) for p in range(PLANES + 1)]
            for p in range(PLANES):
                gains[p] = gains[p] + (capped[p] - capped[p + 1])

        def lift(slot, back_slot, put_odd):
            values = [lifted[slot, r, span(group)] for r in range(16)]
            values.append(ahead_recv[slot, span(group)] * has_next_line)
            details = [
                detail(values[2 * i], values[2 * i + 1], values[2 * i + 2]) for i in range(8)
            ]
            if put_odd is not None:
                for i in range(8):
                    put(2 * i + 1, put_odd, details[i])
            if back_slot is None:
                return None
            behind = (back_recv[back_slot, span(group)] - 0.5 * values[0]) * has_prev_line
            chain = [behind] + details
            smooths = [smooth(values[2 * i], chain[i], chain[i + 1]) for i in range(8)]
            return smooths, behind, details[7]

        for q in (0, 2):
            lift(q, None, q)
        for q, back_slot in ((1, 0), (3, 1)):
            smooths, _, _ = lift(q, back_slot, q)
            for i in range(8):
                put(2 * i, q, smooths[i])
        for k, q in ((0, 0), (1, 2)):
            smooths, behind, last = lift(4 + k, 2 + k, None)
            smooths.append((ahead_recv[6 + k, span(group)] + 0.25 * last) * has_next_line)
            details = [
                detail(smooths[2 * i], smooths[2 * i + 1], smooths[2 * i + 2]) for i in range(4)
            ]
            behind_two = (
                back_recv[4 + k, span(group)] + 0.25 * behind - 0.5 * smooths[0]
            ) * has_prev_line
            chain = [behind_two] + details
            for i in range(4):
                put(4 * i, q, smooth(smooths[2 * i], chain[i], chain[i + 1]))
                put(4 * i + 2, q, details[i])

        sums = [
            jnp.broadcast_to(jnp.sum(gains[p], axis=1, keepdims=True), (8, 128))
            for p in range(PLANES)
        ]
        rates = [rate_cols[p, span(group)] for p in range(PLANES)]

        @pl.loop(0, SLOPE_ROWS, unroll=4)
        def _(row):
            slope = slopes[row]
            total = kept_acc[row]
            for p in range(PLANES):
                total = total + jnp.where(sums[p] >= slope * rates[p], rates[p], 0.0)
            kept_acc[row] = total

    out = pltpu.make_async_copy(wave, w_ref, all_sems.at[2])
    out.start()

    kept_rows[...] = jnp.sum(kept_acc[...], axis=1).astype(jnp.int32)
    place = plane_index(line, tm)

    def row_of(ref, index):
        return ref.at[pl.ds(index, 1)]

    for step in PLANE_STEPS:
        to_line, to_tm = plane_peer(step)
        remote(
            row_of(kept_rows, plane_index(to_line, to_tm)),
            row_of(plane_slots, place),
            tree_sems.at[0, 0],
            tree_sems.at[1, 0],
            to_line,
            to_tm,
        ).start()
    plane_slots[pl.ds(place, 1)] = kept_rows[pl.ds(place, 1)]
    settle(plane_slots.at[pl.ds(0, 31)], tree_sems.at[1, 0])
    ring_row[...] = jnp.sum(plane_slots[...], axis=0, keepdims=True)

    for step in RING_STEPS:
        remote(
            ring_row,
            row_of(ring_slots, z),
            tree_sems.at[0, 1],
            tree_sems.at[1, 1],
            lax.rem(line + step * 8, LINES),
            tm,
        ).start()
    ring_slots[pl.ds(z, 1)] = ring_row[...]
    settle(ring_slots.at[pl.ds(0, 15)], tree_sems.at[1, 1])
    kept = jnp.sum(ring_slots[...], axis=0, keepdims=True)
    limit = target_ref[0] * (SHOTS * LINES * BANDS)
    grid_row = lax.broadcasted_iota(jnp.int32, (1, 128), 1) + place * 128
    above = jnp.where((kept > limit) & (grid_row > 0), 1.0, 0.0)
    count_row[...] = jnp.broadcast_to(jnp.sum(above, axis=1, keepdims=True), (1, 128))

    for step in PLANE_STEPS:
        to_line, to_tm = plane_peer(step)
        remote(
            count_row,
            row_of(count_slots, place),
            tree_sems.at[0, 2],
            tree_sems.at[1, 2],
            to_line,
            to_tm,
        ).start()
    count_slots[pl.ds(place, 1)] = count_row[...]
    settle(count_slots.at[pl.ds(0, 31)], tree_sems.at[1, 2])
    chosen = 1.0 + jnp.sum(count_slots[...], axis=0, keepdims=True)
    slope_now = jnp.exp2(slope_floor + chosen * (slope_span / 2**BISECT))
    shrink_ref[...] = jnp.sqrt(slope_now * rate_cols[PLANES] / rate_scale)

    out.wait()
    settle(most, all_sems.at[0])

    @pl.loop(0, GROUPS)
    def _(group):
        for way in range(2):
            time_copy(way, group).wait_send()
            line_copy(way, group).wait_send()

    settle(plane_slots.at[pl.ds(0, 31)], tree_sems.at[0, 0])
    settle(ring_slots.at[pl.ds(0, 15)], tree_sems.at[0, 1])
    settle(count_slots.at[pl.ds(0, 31)], tree_sems.at[0, 2])


def transform(rows, rates, byte_target):
    vmem = pl.BlockSpec(memory_space=pltpu.VMEM)
    hbm = pl.BlockSpec(memory_space=pl.ANY)
    f32 = jnp.float32
    return pl.pallas_call(
        kernel,
        out_shape=[
            jax.ShapeDtypeStruct((ROWS, 128), f32),
            jax.ShapeDtypeStruct((SHOTS, 128), f32),
        ],
        in_specs=[hbm, vmem, pl.BlockSpec(memory_space=pltpu.SMEM)],
        out_specs=[hbm, vmem],
        scratch_shapes=[
            pltpu.VMEM((ROWS, 128), f32),
            pltpu.VMEM((6, 16, SHOTS, 128), f32),
            pltpu.VMEM((ROWS, 128), f32),
            pltpu.VMEM((2, SHOTS, 128), f32),
            pltpu.VMEM((2, SHOTS, 128), f32),
            pltpu.VMEM((8, SHOTS, 128), f32),
            pltpu.VMEM((8, SHOTS, 128), f32),
            pltpu.VMEM((6, SHOTS, 128), f32),
            pltpu.VMEM((6, SHOTS, 128), f32),
            pltpu.VMEM((SLOPE_ROWS, 8, 128), f32),
            pltpu.VMEM((PLANES + 1, SHOTS, 128), f32),
            pltpu.VMEM((SLOPE_ROWS, 8, 128), f32),
            pltpu.VMEM((SLOPE_ROWS, 128), jnp.int32),
            pltpu.VMEM((SLOPE_ROWS, 128), jnp.int32),
            pltpu.VMEM((1, 128), jnp.int32),
            pltpu.VMEM((16, 128), jnp.int32),
            pltpu.VMEM((1, 128), f32),
            pltpu.VMEM((32, 128), f32),
            pltpu.SemaphoreType.DMA((3,)),
            pltpu.SemaphoreType.DMA((2, 2, GROUPS)),
            pltpu.SemaphoreType.DMA((2, 2, GROUPS)),
            pltpu.SemaphoreType.DMA((2, 3)),
        ],
        compiler_params=pltpu.CompilerParams(
            collective_id=1, has_side_effects=True, vmem_limit_bytes=24 * 2**20
        ),
        name="transform",
    )(rows, rates, byte_target)


def body(traces, rates, byte_target):
    width = traces.shape[3]
    rows = traces.reshape(ROWS, width)
    wave, shrink = transform(rows, rates.reshape(PLANES, SHOTS), byte_target)
    wavelet = wave.reshape(SHOTS, 16, 4, width)
    shrink_by = shrink[:, None, None, :]
    return wavelet - jnp.clip(wavelet, -shrink_by, shrink_by)


def solution(mesh):
    return jax.shard_map(
        body,
        mesh=mesh,
        in_specs=(P("line", None, None, "tm"), P("line", "tm", None, None), P()),
        out_specs=P(None, "line", None, "tm"),
        check_vma=False,
    )
```

```python
import jax
import jax.numpy as jnp
from jax import lax
from jax.experimental import pallas as pl
from jax.experimental.pallas import tpu as pltpu
from jax.sharding import PartitionSpec as P

PLANES = 8
BISECT = 12
LINES = 128
BANDS = 4
SHOTS = 32
GROUPS = 4
ROWS = 2048
FIRST = 17
SLOPE_ROWS = 2**BISECT // 128
MESH = pl.DeviceIdType.MESH

slope_floor = -12.0
slope_span = 32.0
rate_scale = 65536.0

PLANE_STEPS = sorted(
    [(dx, dc, dy) for dx in range(4) for dc in range(2) for dy in range(4)][1:],
    key=lambda s: (-(min(s[0], 4 - s[0]) + min(s[2], 4 - s[2])), s),
)
RING_STEPS = sorted(range(1, 16), key=lambda s: -min(s, 16 - s))


def remote(src, dst, ssem, rsem, line, tm):
    return pltpu.make_async_remote_copy(
        src_ref=src,
        dst_ref=dst,
        send_sem=ssem,
        recv_sem=rsem,
        device_id=(line, tm),
        device_id_type=MESH,
    )


def settle(ref, sem):
    pltpu.make_async_copy(ref, ref, sem).wait()


def detail(even_part, odd_part, ahead_even):
    return odd_part - 0.5 * (even_part + ahead_even)


def smooth(even_part, behind, details):
    return even_part + 0.25 * (behind + details)


def kernel(
    x_ref,
    rates_ref,
    target_ref,
    w_ref,
    shrink_ref,
    local,
    held,
    lifted,
    wave,
    rim_own,
    rim_bands,
    rim_merged,
    rim_plane,
    rim_ring,
    rims,
    ahead_send,
    ahead_recv,
    back_send,
    back_recv,
    rate_table,
    slopes,
    rate_cols,
    kept_acc,
    kept_rows,
    plane_slots,
    ring_row,
    ring_slots,
    count_row,
    count_slots,
    own_sems,
    send_sem,
    arrive_sems,
    rim_sems,
    line_sems,
    tree_sems,
):
    line = lax.axis_index("line")
    tm = lax.axis_index("tm")
    z = line // 8
    x = (line // 2) % 4
    core = line % 2
    spot = line % 8

    def plane_peer(step):
        dx, dc, dy = step
        peer_x = lax.rem(x + dx, 4)
        peer_core = lax.rem(core + dc, 2)
        return z * 8 + peer_x * 2 + peer_core, lax.rem(tm + dy, 4)

    def plane_index(line_at, tm_at):
        return (line_at % 8) * 4 + tm_at

    def span(group):
        return pl.ds(pl.multiple_of(group * 8, 8), 8)

    def row_of(ref, index):
        return ref.at[pl.ds(index, 1)]

    fetch = pltpu.make_async_copy(x_ref, local, own_sems.at[0])
    fetch.start()
    fetch_rates = pltpu.make_async_copy(rates_ref, rate_table, own_sems.at[1])
    fetch_rates.start()

    up = lax.rem(tm + 1, 4)
    down = lax.rem(tm + 3, 4)
    bar = pltpu.get_barrier_semaphore()

    @pl.loop(0, 15)
    def _(i):
        near = 8 - (i + 1) // 2
        step = jnp.where(i % 2 == 0, near, 16 - near)
        plane = lax.rem(z + step, 16) * 8
        for k in range(8):
            pl.semaphore_signal(bar, inc=1, device_id=(plane + k, tm), device_id_type=MESH)

    for k in range(1, 8):
        pl.semaphore_signal(
            bar, inc=1, device_id=(z * 8 + lax.rem(spot + k, 8), tm), device_id_type=MESH
        )
    for to in (up, down):
        pl.semaphore_signal(bar, inc=1, device_id=(line, to), device_id_type=MESH)

    lane = lax.broadcasted_iota(jnp.int32, (8, 128), 1)
    sub = lax.broadcasted_iota(jnp.int32, (8, 128), 0)
    fetch.wait()

    @pl.loop(0, 16)
    def _(plane):
        total = jnp.zeros((8, 128), jnp.float32)
        for block in range(4):
            p0, p1, p2, p3 = [
                local[pl.ds(plane * 128 + block * 32 + q, 8, stride=4), :] for q in range(4)
            ]
            d1 = detail(p0, p1, p2)
            d3 = detail(p2, p3, pltpu.roll(p0, 127, 1))
            s0 = smooth(p0, pltpu.roll(d3, 1, 1), d1)
            rim_detail = p3 - 0.5 * p2
            rim_second = p2 + 0.25 * d1 - 0.5 * s0
            rim_smooth = p0 + 0.25 * d1
            columns = (
                rim_detail[:, 127:128],
                rim_second[:, 127:128],
                p0[:, 0:1],
                rim_smooth[:, 0:1],
            )
            for v, column in enumerate(columns):
                at = (sub + block * 8) * 4 + v
                total = jnp.where(lane == at, jnp.broadcast_to(column, (8, 128)), total)
        rim_own[pl.ds(plane, 1), :] = jnp.sum(total, axis=0, keepdims=True)

    pl.semaphore_wait(bar, LINES + 1)

    band_up = remote(rim_own, rim_bands.at[0], rim_sems.at[0, 0], rim_sems.at[1, 0], line, up)
    band_down = remote(rim_own, rim_bands.at[1], rim_sems.at[0, 1], rim_sems.at[1, 1], line, down)
    band_up.start()
    band_down.start()

    mine = held.at[pl.ds(pl.multiple_of(line * 16, 16), 16)]
    pltpu.make_async_copy(
        x_ref.at[pl.ds(pl.multiple_of(line * 16, 16), 16)], mine, arrive_sems.at[z // 4]
    ).start()

    def scatter(first, last):
        @pl.loop(first, last)
        def _(i):
            to = lax.rem(line + i, LINES)
            remote(
                x_ref.at[pl.ds(pl.multiple_of(to * 16, 16), 16)],
                mine,
                send_sem.at[0],
                arrive_sems.at[z // 4],
                to,
                tm,
            ).start()

    scatter(1, FIRST)

    band_up.wait_recv()
    band_down.wait_recv()
    lane16 = lax.broadcasted_iota(jnp.int32, (16, 128), 1)
    rim_merged[...] = jnp.where(lane16 % 4 < 2, rim_bands[0], rim_bands[1])
    for step in RING_STEPS:
        to = lax.rem(z + step, 16)
        remote(
            row_of(rim_merged, to),
            row_of(rim_ring, z),
            rim_sems.at[0, 3],
            rim_sems.at[1, 3],
            to * 8 + spot,
            tm,
        ).start()
    rim_ring[pl.ds(z, 1), :] = rim_merged[pl.ds(z, 1), :]

    scatter(FIRST, LINES)

    fetch_rates.wait()
    for row in range(SLOPE_ROWS):
        grid_index = (lane + row * 128).astype(jnp.float32)
        slopes[row] = jnp.exp2(slope_floor + grid_index * (slope_span / 2**BISECT))
        kept_acc[row] = jnp.zeros((8, 128), jnp.float32)
    for group in range(GROUPS):
        total = jnp.zeros((8, 128), jnp.float32)
        for plane in range(PLANES):
            rate_row = rate_table[plane : plane + 1, :].astype(jnp.float32)
            picked = jnp.where(
                lane[:, :SHOTS] == sub[:, :SHOTS] + group * 8,
                jnp.broadcast_to(rate_row, (8, SHOTS)),
                0.0,
            )
            column = jnp.broadcast_to(jnp.sum(picked, axis=1, keepdims=True), (8, 128))
            rate_cols[plane, group * 8 : group * 8 + 8] = column
            total = total + column
        rate_cols[PLANES, group * 8 : group * 8 + 8] = total

    settle(rim_ring.at[pl.ds(0, 15)], rim_sems.at[1, 3])
    for k in range(1, 8):
        remote(
            rim_ring,
            rim_plane.at[spot],
            rim_sems.at[0, 2],
            rim_sems.at[1, 2],
            z * 8 + lax.rem(spot + k, 8),
            tm,
        ).start()
    rim_plane[spot] = rim_ring[...]
    settle(rim_plane.at[pl.ds(0, 7)], rim_sems.at[1, 2])
    packed = jnp.zeros((16, 128), jnp.float32)
    for k in range(8):
        turned = pltpu.roll(rim_plane[k], lax.rem((k + 8 - spot) * 16, 128), 1)
        packed = jnp.where(lane16 // 16 == k, turned, packed)

    rims[pl.ds(0, 16, stride=2), :] = packed
    rims[pl.ds(1, 16, stride=2), :] = pltpu.roll(packed, 64, 1)

    has_prev_band = jnp.where(tm > 0, 1.0, 0.0)
    has_next_band = jnp.where(tm < BANDS - 1, 1.0, 0.0)
    has_prev_line = jnp.where(line > 0, 1.0, 0.0)
    has_next_line = jnp.where(line < LINES - 1, 1.0, 0.0)
    line_up = lax.rem(line + 1, LINES)
    line_down = lax.rem(line + LINES - 1, LINES)

    def line_copy(way, group):
        if way == 0:
            return remote(
                ahead_send.at[:, span(group)],
                ahead_recv.at[:, span(group)],
                line_sems.at[0, 0, group],
                line_sems.at[1, 0, group],
                line_down,
                tm,
            )
        return remote(
            back_send.at[:, span(group)],
            back_recv.at[:, span(group)],
            line_sems.at[0, 1, group],
            line_sems.at[1, 1, group],
            line_up,
            tm,
        )

    def group_at(turn):
        return lax.rem(z // 4 + 3 - turn + GROUPS, GROUPS)

    @pl.loop(0, GROUPS)
    def _(turn):
        group = group_at(turn)
        settle(held.at[pl.ds(0, ROWS // GROUPS)], arrive_sems.at[group])
        rim = rims[span(group)]
        low = []
        high = []
        one = []
        three = []
        for r in range(16):
            at = 4 * r
            p0, p1, p2, p3 = [
                held[pl.ds(group * 512 + r * 4 + q, 8, stride=64), :] for q in range(4)
            ]
            d1 = detail(p0, p1, p2)
            ahead = jnp.where(
                lane == 127,
                pltpu.roll(rim, 125 - at, 1) * has_next_band,
                pltpu.roll(p0, 127, 1),
            )
            d3 = detail(p2, p3, ahead)
            rim_detail = pltpu.roll(rim, 128 - at, 1) if at else rim
            d3_prev = (rim_detail - 0.5 * p0) * has_prev_band
            s0 = smooth(p0, jnp.where(lane == 0, d3_prev, pltpu.roll(d3, 1, 1)), d1)
            s2 = smooth(p2, d1, d3)
            next_s0 = (pltpu.roll(rim, 124 - at, 1) + 0.25 * d3) * has_next_band
            second = detail(s0, s2, jnp.where(lane == 127, next_s0, pltpu.roll(s0, 127, 1)))
            rim_second = pltpu.roll(rim, 127 - at, 1)
            second_prev = (rim_second + 0.25 * d3_prev - 0.5 * s0) * has_prev_band
            first = smooth(
                s0, jnp.where(lane == 0, second_prev, pltpu.roll(second, 1, 1)), second
            )
            for slot, value in enumerate((s0, d1, s2, d3, first, second)):
                lifted[slot, r, span(group)] = value
            if r == 0:
                for slot, value in enumerate((s0, d1, s2, d3, first, second)):
                    ahead_send[slot, span(group)] = value
            one.append(d1)
            three.append(d3)
            low.append(first)
            high.append(second)
        for slot, value in enumerate((low, high)):
            ahead_send[6 + slot, span(group)] = value[0] + 0.25 * detail(value[0], value[1], value[2])
            d5 = detail(value[10], value[11], value[12])
            d6 = detail(value[12], value[13], value[14])
            s6 = smooth(value[12], d5, d6)
            back_send[4 + slot, span(group)] = value[14] + 0.25 * d6 - 0.5 * s6
        for slot, value in enumerate((one, three, low, high)):
            back_send[slot, span(group)] = value[15] - 0.5 * value[14]
        line_copy(0, group).start()
        line_copy(1, group).start()

    @pl.loop(0, GROUPS)
    def _(turn):
        group = group_at(turn)
        line_copy(0, group).wait_recv()
        line_copy(1, group).wait_recv()
        gains = [jnp.zeros((8, 128), jnp.float32) for _ in range(PLANES)]

        def put(r, q, value):
            wave[pl.ds(group * 512 + r * 4 + q, 8, stride=64), :] = value
            square = value * value
            capped = [jnp.minimum(square, 4.0 ** (4 - p)) for p in range(PLANES + 1)]
            for p in range(PLANES):
                gains[p] = gains[p] + (capped[p] - capped[p + 1])

        def lift(slot, back_slot, put_odd):
            values = [lifted[slot, r, span(group)] for r in range(16)]
            values.append(ahead_recv[slot, span(group)] * has_next_line)
            details = [
                detail(values[2 * i], values[2 * i + 1], values[2 * i + 2]) for i in range(8)
            ]
            if put_odd is not None:
                for i in range(8):
                    put(2 * i + 1, put_odd, details[i])
            if back_slot is None:
                return None
            behind = (back_recv[back_slot, span(group)] - 0.5 * values[0]) * has_prev_line
            chain = [behind] + details
            smooths = [smooth(values[2 * i], chain[i], chain[i + 1]) for i in range(8)]
            return smooths, behind, details[7]

        for q in (0, 2):
            lift(q, None, q)
        for q, back_slot in ((1, 0), (3, 1)):
            smooths, _, _ = lift(q, back_slot, q)
            for i in range(8):
                put(2 * i, q, smooths[i])
        for k, q in ((0, 0), (1, 2)):
            smooths, behind, last = lift(4 + k, 2 + k, None)
            smooths.append((ahead_recv[6 + k, span(group)] + 0.25 * last) * has_next_line)
            details = [
                detail(smooths[2 * i], smooths[2 * i + 1], smooths[2 * i + 2]) for i in range(4)
            ]
            behind_two = (
                back_recv[4 + k, span(group)] + 0.25 * behind - 0.5 * smooths[0]
            ) * has_prev_line
            chain = [behind_two] + details
            for i in range(4):
                put(4 * i, q, smooth(smooths[2 * i], chain[i], chain[i + 1]))
                put(4 * i + 2, q, details[i])

        sums = [
            jnp.broadcast_to(jnp.sum(gains[p], axis=1, keepdims=True), (8, 128))
            for p in range(PLANES)
        ]
        rates = [rate_cols[p, span(group)] for p in range(PLANES)]

        @pl.loop(0, SLOPE_ROWS, unroll=4)
        def _(row):
            slope = slopes[row]
            total = kept_acc[row]
            for p in range(PLANES):
                total = total + jnp.where(sums[p] >= slope * rates[p], rates[p], 0.0)
            kept_acc[row] = total

    out = pltpu.make_async_copy(wave, w_ref, own_sems.at[0])
    out.start()

    kept_rows[...] = jnp.sum(kept_acc[...], axis=1).astype(jnp.int32)
    place = plane_index(line, tm)

    for step in PLANE_STEPS:
        to_line, to_tm = plane_peer(step)
        remote(
            row_of(kept_rows, plane_index(to_line, to_tm)),
            row_of(plane_slots, place),
            tree_sems.at[0, 0],
            tree_sems.at[1, 0],
            to_line,
            to_tm,
        ).start()
    plane_slots[pl.ds(place, 1)] = kept_rows[pl.ds(place, 1)]
    settle(plane_slots.at[pl.ds(0, 31)], tree_sems.at[1, 0])
    ring_row[...] = jnp.sum(plane_slots[...], axis=0, keepdims=True)

    for step in RING_STEPS:
        remote(
            ring_row,
            row_of(ring_slots, z),
            tree_sems.at[0, 1],
            tree_sems.at[1, 1],
            lax.rem(line + step * 8, LINES),
            tm,
        ).start()
    ring_slots[pl.ds(z, 1)] = ring_row[...]
    settle(ring_slots.at[pl.ds(0, 15)], tree_sems.at[1, 1])
    kept = jnp.sum(ring_slots[...], axis=0, keepdims=True)
    limit = target_ref[0] * (SHOTS * LINES * BANDS)
    grid_row = lax.broadcasted_iota(jnp.int32, (1, 128), 1) + place * 128
    above = jnp.where((kept > limit) & (grid_row > 0), 1.0, 0.0)
    count_row[...] = jnp.broadcast_to(jnp.sum(above, axis=1, keepdims=True), (1, 128))

    for step in PLANE_STEPS:
        to_line, to_tm = plane_peer(step)
        remote(
            count_row,
            row_of(count_slots, place),
            tree_sems.at[0, 2],
            tree_sems.at[1, 2],
            to_line,
            to_tm,
        ).start()
    count_slots[pl.ds(place, 1)] = count_row[...]
    settle(count_slots.at[pl.ds(0, 31)], tree_sems.at[1, 2])
    chosen = 1.0 + jnp.sum(count_slots[...], axis=0, keepdims=True)
    slope_now = jnp.exp2(slope_floor + chosen * (slope_span / 2**BISECT))
    shrink_ref[...] = jnp.sqrt(slope_now * rate_cols[PLANES] / rate_scale)

    out.wait()
    settle(held.at[pl.ds(0, ROWS - 16)], send_sem.at[0])
    band_up.wait_send()
    band_down.wait_send()
    settle(rim_plane.at[pl.ds(0, 7)], rim_sems.at[0, 2])
    settle(rim_ring.at[pl.ds(0, 15)], rim_sems.at[0, 3])

    @pl.loop(0, GROUPS)
    def _(group):
        for way in range(2):
            line_copy(way, group).wait_send()

    settle(plane_slots.at[pl.ds(0, 31)], tree_sems.at[0, 0])
    settle(ring_slots.at[pl.ds(0, 15)], tree_sems.at[0, 1])
    settle(count_slots.at[pl.ds(0, 31)], tree_sems.at[0, 2])


def transform(rows, rates, byte_target):
    vmem = pl.BlockSpec(memory_space=pltpu.VMEM)
    hbm = pl.BlockSpec(memory_space=pl.ANY)
    rows, rates = [pltpu.with_memory_space_constraint(a, pltpu.HBM) for a in (rows, rates)]
    f32 = jnp.float32
    return pl.pallas_call(
        kernel,
        out_shape=[
            jax.ShapeDtypeStruct((ROWS, 128), f32),
            jax.ShapeDtypeStruct((SHOTS, 128), f32),
        ],
        in_specs=[hbm, hbm, pl.BlockSpec(memory_space=pltpu.SMEM)],
        out_specs=[hbm, vmem],
        scratch_shapes=[
            pltpu.VMEM((ROWS, 128), f32),
            pltpu.VMEM((ROWS, 128), f32),
            pltpu.VMEM((6, 16, SHOTS, 128), f32),
            pltpu.VMEM((ROWS, 128), f32),
            pltpu.VMEM((16, 128), f32),
            pltpu.VMEM((2, 16, 128), f32),
            pltpu.VMEM((16, 128), f32),
            pltpu.VMEM((8, 16, 128), f32),
            pltpu.VMEM((16, 128), f32),
            pltpu.VMEM((SHOTS, 128), f32),
            pltpu.VMEM((8, SHOTS, 128), f32),
            pltpu.VMEM((8, SHOTS, 128), f32),
            pltpu.VMEM((6, SHOTS, 128), f32),
            pltpu.VMEM((6, SHOTS, 128), f32),
            pltpu.VMEM((PLANES, SHOTS), jnp.int32),
            pltpu.VMEM((SLOPE_ROWS, 8, 128), f32),
            pltpu.VMEM((PLANES + 1, SHOTS, 128), f32),
            pltpu.VMEM((SLOPE_ROWS, 8, 128), f32),
            pltpu.VMEM((SLOPE_ROWS, 128), jnp.int32),
            pltpu.VMEM((SLOPE_ROWS, 128), jnp.int32),
            pltpu.VMEM((1, 128), jnp.int32),
            pltpu.VMEM((16, 128), jnp.int32),
            pltpu.VMEM((1, 128), f32),
            pltpu.VMEM((32, 128), f32),
            pltpu.SemaphoreType.DMA((2,)),
            pltpu.SemaphoreType.DMA((1,)),
            pltpu.SemaphoreType.DMA((GROUPS,)),
            pltpu.SemaphoreType.DMA((2, 4)),
            pltpu.SemaphoreType.DMA((2, 2, GROUPS)),
            pltpu.SemaphoreType.DMA((2, 3)),
        ],
        compiler_params=pltpu.CompilerParams(
            collective_id=1, has_side_effects=True, vmem_limit_bytes=24 * 2**20
        ),
        name="transform",
    )(rows, rates, byte_target)


def body(traces, rates, byte_target):
    width = traces.shape[3]
    rows = traces.reshape(ROWS, width)
    wave, shrink = transform(rows, rates.reshape(PLANES, SHOTS), byte_target)
    wavelet = wave.reshape(SHOTS, 16, 4, width)
    shrink_by = shrink[:, None, None, :]
    return wavelet - jnp.clip(wavelet, -shrink_by, shrink_by)


def solution(mesh):
    return jax.shard_map(
        body,
        mesh=mesh,
        in_specs=(P("line", None, None, "tm"), P("line", "tm", None, None), P()),
        out_specs=P(None, "line", None, "tm"),
        check_vma=False,
    )
```

```python
import jax
import jax.numpy as jnp
from jax import lax
from jax.experimental import pallas as pl
from jax.experimental.pallas import tpu as pltpu
from jax.sharding import PartitionSpec as P

PLANES = 8
BISECT = 12
LINES = 128
BANDS = 4
SHOTS = 32
GROUPS = 4
ROWS = 2048
FIRST = 32
SECOND = 112
SLOPE_ROWS = 2**BISECT // 128
MESH = pl.DeviceIdType.MESH

slope_floor = -12.0
slope_span = 32.0
rate_scale = 65536.0

PLANE_STEPS = sorted(
    [(dx, dc, dy) for dx in range(4) for dc in range(2) for dy in range(4)][1:],
    key=lambda s: (-(min(s[0], 4 - s[0]) + min(s[2], 4 - s[2])), s),
)
RING_STEPS = sorted(range(1, 16), key=lambda s: -min(s, 16 - s))


def remote(src, dst, ssem, rsem, line, tm):
    return pltpu.make_async_remote_copy(
        src_ref=src,
        dst_ref=dst,
        send_sem=ssem,
        recv_sem=rsem,
        device_id=(line, tm),
        device_id_type=MESH,
    )


def settle(ref, sem):
    pltpu.make_async_copy(ref, ref, sem).wait()


def detail(even_part, odd_part, ahead_even):
    return odd_part - 0.5 * (even_part + ahead_even)


def smooth(even_part, behind, details):
    return even_part + 0.25 * (behind + details)


def kernel(
    x_ref,
    rates_ref,
    target_ref,
    w_ref,
    shrink_ref,
    local,
    held,
    lifted,
    wave,
    rim_own,
    rim_bands,
    rim_merged,
    rim_plane,
    rim_ring,
    rims,
    ahead_send,
    ahead_recv,
    back_send,
    back_recv,
    rate_table,
    slopes,
    rate_cols,
    kept_acc,
    kept_rows,
    plane_slots,
    ring_row,
    ring_slots,
    count_row,
    count_slots,
    own_sems,
    send_sem,
    arrive_sems,
    rim_sems,
    line_sems,
    tree_sems,
):
    line = lax.axis_index("line")
    tm = lax.axis_index("tm")
    z = line // 8
    x = (line // 2) % 4
    core = line % 2
    spot = line % 8

    def plane_peer(step):
        dx, dc, dy = step
        peer_x = lax.rem(x + dx, 4)
        peer_core = lax.rem(core + dc, 2)
        return z * 8 + peer_x * 2 + peer_core, lax.rem(tm + dy, 4)

    def plane_index(line_at, tm_at):
        return (line_at % 8) * 4 + tm_at

    def span(group):
        return pl.ds(pl.multiple_of(group * 8, 8), 8)

    def row_of(ref, index):
        return ref.at[pl.ds(index, 1)]

    fetch = pltpu.make_async_copy(x_ref, local, own_sems.at[0])
    fetch.start()
    fetch_rates = pltpu.make_async_copy(rates_ref, rate_table, own_sems.at[1])
    fetch_rates.start()

    up = lax.rem(tm + 1, 4)
    down = lax.rem(tm + 3, 4)
    bar = pltpu.get_barrier_semaphore()

    @pl.loop(0, 15)
    def _(i):
        near = 8 - (i + 1) // 2
        step = jnp.where(i % 2 == 0, near, 16 - near)
        plane = lax.rem(z + step, 16) * 8
        for k in range(8):
            pl.semaphore_signal(bar, inc=1, device_id=(plane + k, tm), device_id_type=MESH)

    for k in range(1, 8):
        pl.semaphore_signal(
            bar, inc=1, device_id=(z * 8 + lax.rem(spot + k, 8), tm), device_id_type=MESH
        )
    for to in (up, down):
        pl.semaphore_signal(bar, inc=1, device_id=(line, to), device_id_type=MESH)

    lane = lax.broadcasted_iota(jnp.int32, (8, 128), 1)
    sub = lax.broadcasted_iota(jnp.int32, (8, 128), 0)
    fetch.wait()

    @pl.loop(0, 16)
    def _(plane):
        total = jnp.zeros((8, 128), jnp.float32)
        for block in range(4):
            p0, p1, p2, p3 = [
                local[pl.ds(plane * 128 + block * 32 + q, 8, stride=4), :] for q in range(4)
            ]
            d1 = detail(p0, p1, p2)
            d3 = detail(p2, p3, pltpu.roll(p0, 127, 1))
            s0 = smooth(p0, pltpu.roll(d3, 1, 1), d1)
            rim_detail = p3 - 0.5 * p2
            rim_second = p2 + 0.25 * d1 - 0.5 * s0
            rim_smooth = p0 + 0.25 * d1
            columns = (
                rim_detail[:, 127:128],
                rim_second[:, 127:128],
                p0[:, 0:1],
                rim_smooth[:, 0:1],
            )
            for v, column in enumerate(columns):
                at = (sub + block * 8) * 4 + v
                total = jnp.where(lane == at, jnp.broadcast_to(column, (8, 128)), total)
        rim_own[pl.ds(plane, 1), :] = jnp.sum(total, axis=0, keepdims=True)

    pl.semaphore_wait(bar, LINES + 1)

    band_up = remote(rim_own, rim_bands.at[0], rim_sems.at[0, 0], rim_sems.at[1, 0], line, up)
    band_down = remote(rim_own, rim_bands.at[1], rim_sems.at[0, 1], rim_sems.at[1, 1], line, down)
    band_up.start()
    band_down.start()

    mine = held.at[pl.ds(pl.multiple_of(line * 16, 16), 16)]
    pltpu.make_async_copy(
        x_ref.at[pl.ds(pl.multiple_of(line * 16, 16), 16)], mine, arrive_sems.at[z // 4]
    ).start()

    def scatter(first, last):
        @pl.loop(first, last)
        def _(i):
            near = (i + 1) // 2
            to = lax.rem(line + jnp.where(i % 2 == 0, 64 - near, 64 + near), LINES)
            remote(
                x_ref.at[pl.ds(pl.multiple_of(to * 16, 16), 16)],
                mine,
                send_sem.at[0],
                arrive_sems.at[z // 4],
                to,
                tm,
            ).start()

    scatter(0, FIRST)

    band_up.wait_recv()
    band_down.wait_recv()
    lane16 = lax.broadcasted_iota(jnp.int32, (16, 128), 1)
    rim_merged[...] = jnp.where(lane16 % 4 < 2, rim_bands[0], rim_bands[1])
    for step in RING_STEPS:
        to = lax.rem(z + step, 16)
        remote(
            row_of(rim_merged, to),
            row_of(rim_ring, z),
            rim_sems.at[0, 3],
            rim_sems.at[1, 3],
            to * 8 + spot,
            tm,
        ).start()
    rim_ring[pl.ds(z, 1), :] = rim_merged[pl.ds(z, 1), :]

    scatter(FIRST, SECOND)

    settle(rim_ring.at[pl.ds(0, 15)], rim_sems.at[1, 3])
    for k in range(1, 8):
        remote(
            rim_ring,
            rim_plane.at[spot],
            rim_sems.at[0, 2],
            rim_sems.at[1, 2],
            z * 8 + lax.rem(spot + k, 8),
            tm,
        ).start()
    rim_plane[spot] = rim_ring[...]

    scatter(SECOND, LINES - 1)

    fetch_rates.wait()
    for row in range(SLOPE_ROWS):
        grid_index = (lane + row * 128).astype(jnp.float32)
        slopes[row] = jnp.exp2(slope_floor + grid_index * (slope_span / 2**BISECT))
        kept_acc[row] = jnp.zeros((8, 128), jnp.float32)
    for group in range(GROUPS):
        total = jnp.zeros((8, 128), jnp.float32)
        for plane in range(PLANES):
            rate_row = rate_table[plane : plane + 1, :].astype(jnp.float32)
            picked = jnp.where(
                lane[:, :SHOTS] == sub[:, :SHOTS] + group * 8,
                jnp.broadcast_to(rate_row, (8, SHOTS)),
                0.0,
            )
            column = jnp.broadcast_to(jnp.sum(picked, axis=1, keepdims=True), (8, 128))
            rate_cols[plane, group * 8 : group * 8 + 8] = column
            total = total + column
        rate_cols[PLANES, group * 8 : group * 8 + 8] = total

    settle(rim_plane.at[pl.ds(0, 7)], rim_sems.at[1, 2])
    packed = jnp.zeros((16, 128), jnp.float32)
    for k in range(8):
        turned = pltpu.roll(rim_plane[k], lax.rem((k + 8 - spot) * 16, 128), 1)
        packed = jnp.where(lane16 // 16 == k, turned, packed)

    rims[pl.ds(0, 16, stride=2), :] = packed
    rims[pl.ds(1, 16, stride=2), :] = pltpu.roll(packed, 64, 1)

    has_prev_band = jnp.where(tm > 0, 1.0, 0.0)
    has_next_band = jnp.where(tm < BANDS - 1, 1.0, 0.0)
    has_prev_line = jnp.where(line > 0, 1.0, 0.0)
    has_next_line = jnp.where(line < LINES - 1, 1.0, 0.0)
    line_up = lax.rem(line + 1, LINES)
    line_down = lax.rem(line + LINES - 1, LINES)

    def line_copy(way, group):
        if way == 0:
            return remote(
                ahead_send.at[:, span(group)],
                ahead_recv.at[:, span(group)],
                line_sems.at[0, 0, group],
                line_sems.at[1, 0, group],
                line_down,
                tm,
            )
        return remote(
            back_send.at[:, span(group)],
            back_recv.at[:, span(group)],
            line_sems.at[0, 1, group],
            line_sems.at[1, 1, group],
            line_up,
            tm,
        )

    def group_at(turn):
        return lax.rem(z // 4 + jnp.where(turn == 0, 2, jnp.where(turn == 1, 1, jnp.where(turn == 2, 3, 0))), GROUPS)

    @pl.loop(0, GROUPS)
    def _(turn):
        group = group_at(turn)
        settle(held.at[pl.ds(0, ROWS // GROUPS)], arrive_sems.at[group])
        rim = rims[span(group)]
        low = []
        high = []
        one = []
        three = []
        for r in range(16):
            at = 4 * r
            p0, p1, p2, p3 = [
                held[pl.ds(group * 512 + r * 4 + q, 8, stride=64), :] for q in range(4)
            ]
            d1 = detail(p0, p1, p2)
            ahead = jnp.where(
                lane == 127,
                pltpu.roll(rim, 125 - at, 1) * has_next_band,
                pltpu.roll(p0, 127, 1),
            )
            d3 = detail(p2, p3, ahead)
            rim_detail = pltpu.roll(rim, 128 - at, 1) if at else rim
            d3_prev = (rim_detail - 0.5 * p0) * has_prev_band
            s0 = smooth(p0, jnp.where(lane == 0, d3_prev, pltpu.roll(d3, 1, 1)), d1)
            s2 = smooth(p2, d1, d3)
            next_s0 = (pltpu.roll(rim, 124 - at, 1) + 0.25 * d3) * has_next_band
            second = detail(s0, s2, jnp.where(lane == 127, next_s0, pltpu.roll(s0, 127, 1)))
            rim_second = pltpu.roll(rim, 127 - at, 1)
            second_prev = (rim_second + 0.25 * d3_prev - 0.5 * s0) * has_prev_band
            first = smooth(
                s0, jnp.where(lane == 0, second_prev, pltpu.roll(second, 1, 1)), second
            )
            for slot, value in enumerate((s0, d1, s2, d3, first, second)):
                lifted[slot, r, span(group)] = value
            if r == 0:
                for slot, value in enumerate((s0, d1, s2, d3, first, second)):
                    ahead_send[slot, span(group)] = value
            one.append(d1)
            three.append(d3)
            low.append(first)
            high.append(second)
        for slot, value in enumerate((low, high)):
            ahead_send[6 + slot, span(group)] = value[0] + 0.25 * detail(value[0], value[1], value[2])
            d5 = detail(value[10], value[11], value[12])
            d6 = detail(value[12], value[13], value[14])
            s6 = smooth(value[12], d5, d6)
            back_send[4 + slot, span(group)] = value[14] + 0.25 * d6 - 0.5 * s6
        for slot, value in enumerate((one, three, low, high)):
            back_send[slot, span(group)] = value[15] - 0.5 * value[14]
        line_copy(0, group).start()
        line_copy(1, group).start()

    @pl.loop(0, GROUPS)
    def _(turn):
        group = group_at(turn)
        line_copy(0, group).wait_recv()
        line_copy(1, group).wait_recv()
        gains = [jnp.zeros((8, 128), jnp.float32) for _ in range(PLANES)]

        def put(r, q, value):
            wave[pl.ds(group * 512 + r * 4 + q, 8, stride=64), :] = value
            square = value * value
            capped = [jnp.minimum(square, 4.0 ** (4 - p)) for p in range(PLANES + 1)]
            for p in range(PLANES):
                gains[p] = gains[p] + (capped[p] - capped[p + 1])

        def lift(slot, back_slot, put_odd):
            values = [lifted[slot, r, span(group)] for r in range(16)]
            values.append(ahead_recv[slot, span(group)] * has_next_line)
            details = [
                detail(values[2 * i], values[2 * i + 1], values[2 * i + 2]) for i in range(8)
            ]
            if put_odd is not None:
                for i in range(8):
                    put(2 * i + 1, put_odd, details[i])
            if back_slot is None:
                return None
            behind = (back_recv[back_slot, span(group)] - 0.5 * values[0]) * has_prev_line
            chain = [behind] + details
            smooths = [smooth(values[2 * i], chain[i], chain[i + 1]) for i in range(8)]
            return smooths, behind, details[7]

        for q in (0, 2):
            lift(q, None, q)
        for q, back_slot in ((1, 0), (3, 1)):
            smooths, _, _ = lift(q, back_slot, q)
            for i in range(8):
                put(2 * i, q, smooths[i])
        for k, q in ((0, 0), (1, 2)):
            smooths, behind, last = lift(4 + k, 2 + k, None)
            smooths.append((ahead_recv[6 + k, span(group)] + 0.25 * last) * has_next_line)
            details = [
                detail(smooths[2 * i], smooths[2 * i + 1], smooths[2 * i + 2]) for i in range(4)
            ]
            behind_two = (
                back_recv[4 + k, span(group)] + 0.25 * behind - 0.5 * smooths[0]
            ) * has_prev_line
            chain = [behind_two] + details
            for i in range(4):
                put(4 * i, q, smooth(smooths[2 * i], chain[i], chain[i + 1]))
                put(4 * i + 2, q, details[i])

        sums = [
            jnp.broadcast_to(jnp.sum(gains[p], axis=1, keepdims=True), (8, 128))
            for p in range(PLANES)
        ]
        rates = [rate_cols[p, span(group)] for p in range(PLANES)]

        @pl.loop(0, SLOPE_ROWS, unroll=4)
        def _(row):
            slope = slopes[row]
            total = kept_acc[row]
            for p in range(PLANES):
                total = total + jnp.where(sums[p] >= slope * rates[p], rates[p], 0.0)
            kept_acc[row] = total

    out = pltpu.make_async_copy(wave, w_ref, own_sems.at[0])
    out.start()

    kept_rows[...] = jnp.sum(kept_acc[...], axis=1).astype(jnp.int32)
    place = plane_index(line, tm)

    for step in PLANE_STEPS:
        to_line, to_tm = plane_peer(step)
        remote(
            row_of(kept_rows, plane_index(to_line, to_tm)),
            row_of(plane_slots, place),
            tree_sems.at[0, 0],
            tree_sems.at[1, 0],
            to_line,
            to_tm,
        ).start()
    plane_slots[pl.ds(place, 1)] = kept_rows[pl.ds(place, 1)]
    settle(plane_slots.at[pl.ds(0, 31)], tree_sems.at[1, 0])
    ring_row[...] = jnp.sum(plane_slots[...], axis=0, keepdims=True)

    for step in RING_STEPS:
        remote(
            ring_row,
            row_of(ring_slots, z),
            tree_sems.at[0, 1],
            tree_sems.at[1, 1],
            lax.rem(line + step * 8, LINES),
            tm,
        ).start()
    ring_slots[pl.ds(z, 1)] = ring_row[...]
    settle(ring_slots.at[pl.ds(0, 15)], tree_sems.at[1, 1])
    kept = jnp.sum(ring_slots[...], axis=0, keepdims=True)
    limit = target_ref[0] * (SHOTS * LINES * BANDS)
    grid_row = lax.broadcasted_iota(jnp.int32, (1, 128), 1) + place * 128
    above = jnp.where((kept > limit) & (grid_row > 0), 1.0, 0.0)
    count_row[...] = jnp.broadcast_to(jnp.sum(above, axis=1, keepdims=True), (1, 128))

    for step in PLANE_STEPS:
        to_line, to_tm = plane_peer(step)
        remote(
            count_row,
            row_of(count_slots, place),
            tree_sems.at[0, 2],
            tree_sems.at[1, 2],
            to_line,
            to_tm,
        ).start()
    count_slots[pl.ds(place, 1)] = count_row[...]
    settle(count_slots.at[pl.ds(0, 31)], tree_sems.at[1, 2])
    chosen = 1.0 + jnp.sum(count_slots[...], axis=0, keepdims=True)
    slope_now = jnp.exp2(slope_floor + chosen * (slope_span / 2**BISECT))
    shrink_ref[...] = jnp.sqrt(slope_now * rate_cols[PLANES] / rate_scale)

    out.wait()
    settle(held.at[pl.ds(0, ROWS - 16)], send_sem.at[0])
    band_up.wait_send()
    band_down.wait_send()
    settle(rim_plane.at[pl.ds(0, 7)], rim_sems.at[0, 2])
    settle(rim_ring.at[pl.ds(0, 15)], rim_sems.at[0, 3])

    @pl.loop(0, GROUPS)
    def _(group):
        for way in range(2):
            line_copy(way, group).wait_send()

    settle(plane_slots.at[pl.ds(0, 31)], tree_sems.at[0, 0])
    settle(ring_slots.at[pl.ds(0, 15)], tree_sems.at[0, 1])
    settle(count_slots.at[pl.ds(0, 31)], tree_sems.at[0, 2])


def transform(rows, rates, byte_target):
    vmem = pl.BlockSpec(memory_space=pltpu.VMEM)
    hbm = pl.BlockSpec(memory_space=pl.ANY)
    rows, rates = [pltpu.with_memory_space_constraint(a, pltpu.HBM) for a in (rows, rates)]
    f32 = jnp.float32
    return pl.pallas_call(
        kernel,
        out_shape=[
            jax.ShapeDtypeStruct((ROWS, 128), f32),
            jax.ShapeDtypeStruct((SHOTS, 128), f32),
        ],
        in_specs=[hbm, hbm, pl.BlockSpec(memory_space=pltpu.SMEM)],
        out_specs=[hbm, vmem],
        scratch_shapes=[
            pltpu.VMEM((ROWS, 128), f32),
            pltpu.VMEM((ROWS, 128), f32),
            pltpu.VMEM((6, 16, SHOTS, 128), f32),
            pltpu.VMEM((ROWS, 128), f32),
            pltpu.VMEM((16, 128), f32),
            pltpu.VMEM((2, 16, 128), f32),
            pltpu.VMEM((16, 128), f32),
            pltpu.VMEM((8, 16, 128), f32),
            pltpu.VMEM((16, 128), f32),
            pltpu.VMEM((SHOTS, 128), f32),
            pltpu.VMEM((8, SHOTS, 128), f32),
            pltpu.VMEM((8, SHOTS, 128), f32),
            pltpu.VMEM((6, SHOTS, 128), f32),
            pltpu.VMEM((6, SHOTS, 128), f32),
            pltpu.VMEM((PLANES, SHOTS), jnp.int32),
            pltpu.VMEM((SLOPE_ROWS, 8, 128), f32),
            pltpu.VMEM((PLANES + 1, SHOTS, 128), f32),
            pltpu.VMEM((SLOPE_ROWS, 8, 128), f32),
            pltpu.VMEM((SLOPE_ROWS, 128), jnp.int32),
            pltpu.VMEM((SLOPE_ROWS, 128), jnp.int32),
            pltpu.VMEM((1, 128), jnp.int32),
            pltpu.VMEM((16, 128), jnp.int32),
            pltpu.VMEM((1, 128), f32),
            pltpu.VMEM((32, 128), f32),
            pltpu.SemaphoreType.DMA((2,)),
            pltpu.SemaphoreType.DMA((1,)),
            pltpu.SemaphoreType.DMA((GROUPS,)),
            pltpu.SemaphoreType.DMA((2, 4)),
            pltpu.SemaphoreType.DMA((2, 2, GROUPS)),
            pltpu.SemaphoreType.DMA((2, 3)),
        ],
        compiler_params=pltpu.CompilerParams(
            collective_id=1, has_side_effects=True, vmem_limit_bytes=24 * 2**20
        ),
        name="transform",
    )(rows, rates, byte_target)


def body(traces, rates, byte_target):
    width = traces.shape[3]
    rows = traces.reshape(ROWS, width)
    wave, shrink = transform(rows, rates.reshape(PLANES, SHOTS), byte_target)
    wavelet = wave.reshape(SHOTS, 16, 4, width)
    shrink_by = shrink[:, None, None, :]
    return wavelet - jnp.clip(wavelet, -shrink_by, shrink_by)


def solution(mesh):
    return jax.shard_map(
        body,
        mesh=mesh,
        in_specs=(P("line", None, None, "tm"), P("line", "tm", None, None), P()),
        out_specs=P(None, "line", None, "tm"),
        check_vma=False,
    )
```

```python
import jax
import jax.numpy as jnp
from jax import lax
from jax.experimental import pallas as pl
from jax.experimental.pallas import tpu as pltpu
from jax.sharding import PartitionSpec as P

PLANES = 8
BISECT = 12
LINES = 128
BANDS = 4
SHOTS = 32
GROUPS = 4
ROWS = 2048
FIRST = 32
SECOND = 112
SLOPE_ROWS = 2**BISECT // 128
MESH = pl.DeviceIdType.MESH

slope_floor = -12.0
slope_span = 32.0
rate_scale = 65536.0

PLANE_STEPS = sorted(
    [(dx, dc, dy) for dx in range(4) for dc in range(2) for dy in range(4)][1:],
    key=lambda s: (-(min(s[0], 4 - s[0]) + min(s[2], 4 - s[2])), s),
)
RING_STEPS = sorted(range(1, 16), key=lambda s: -min(s, 16 - s))


def remote(src, dst, ssem, rsem, line, tm):
    return pltpu.make_async_remote_copy(
        src_ref=src,
        dst_ref=dst,
        send_sem=ssem,
        recv_sem=rsem,
        device_id=(line, tm),
        device_id_type=MESH,
    )


def settle(ref, sem):
    pltpu.make_async_copy(ref, ref, sem).wait()


def wrap(value, count):
    return jnp.where(value >= count, value - count, value)


def detail(even_part, odd_part, ahead_even):
    return odd_part - 0.5 * (even_part + ahead_even)


def smooth(even_part, behind, details):
    return even_part + 0.25 * (behind + details)


def kernel(
    x_ref,
    rates_ref,
    target_ref,
    w_ref,
    shrink_ref,
    local,
    held,
    lifted,
    wave,
    rim_own,
    rim_bands,
    rim_merged,
    rim_plane,
    rim_ring,
    rims,
    ahead_send,
    ahead_recv,
    back_send,
    back_recv,
    rate_table,
    bars,
    edges,
    gain_acc,
    rate_cols,
    kept_acc,
    kept_rows,
    plane_slots,
    ring_row,
    ring_slots,
    count_row,
    count_slots,
    own_sems,
    send_sem,
    arrive_sems,
    rim_sems,
    line_sems,
    tree_sems,
):
    line = lax.axis_index("line")
    tm = lax.axis_index("tm")
    z = line // 8
    x = (line // 2) % 4
    core = line % 2
    spot = line % 8

    peer_x = [(z * 4 + wrap(x + k, 4)) * 2 for k in range(4)]
    peer_core = [core, 1 - core]
    peer_tm = [wrap(tm + k, 4) for k in range(4)]

    def plane_peer(step):
        dx, dc, dy = step
        return peer_x[dx] + peer_core[dc], peer_tm[dy]

    def plane_index(line_at, tm_at):
        return (line_at % 8) * 4 + tm_at

    def span(group):
        return pl.ds(pl.multiple_of(group * 8, 8), 8)

    def row_of(ref, index):
        return ref.at[pl.ds(index, 1)]

    fetch = pltpu.make_async_copy(x_ref, local, own_sems.at[0])
    fetch.start()
    fetch_rates = pltpu.make_async_copy(rates_ref, rate_table, own_sems.at[1])
    fetch_rates.start()

    up, down = peer_tm[1], peer_tm[3]
    bar = pltpu.get_barrier_semaphore()

    @pl.loop(0, 15)
    def _(i):
        near = 8 - (i + 1) // 2
        step = jnp.where(i % 2 == 0, near, 16 - near)
        plane = wrap(z + step, 16) * 8
        for k in range(8):
            pl.semaphore_signal(bar, inc=1, device_id=(plane + k, tm), device_id_type=MESH)

    for k in range(1, 8):
        pl.semaphore_signal(
            bar, inc=1, device_id=(z * 8 + wrap(spot + k, 8), tm), device_id_type=MESH
        )
    for to in (up, down):
        pl.semaphore_signal(bar, inc=1, device_id=(line, to), device_id_type=MESH)

    lane = lax.broadcasted_iota(jnp.int32, (8, 128), 1)
    sub = lax.broadcasted_iota(jnp.int32, (8, 128), 0)
    fetch.wait()

    @pl.loop(0, 16)
    def _(plane):
        total = jnp.zeros((8, 128), jnp.float32)
        for block in range(4):
            p0, p1, p2, p3 = [
                local[pl.ds(plane * 128 + block * 32 + q, 8, stride=4), :] for q in range(4)
            ]
            d1 = detail(p0, p1, p2)
            d3 = detail(p2, p3, pltpu.roll(p0, 127, 1))
            s0 = smooth(p0, pltpu.roll(d3, 1, 1), d1)
            rim_detail = p3 - 0.5 * p2
            rim_second = p2 + 0.25 * d1 - 0.5 * s0
            rim_smooth = p0 + 0.25 * d1
            columns = (
                rim_detail[:, 127:128],
                rim_second[:, 127:128],
                p0[:, 0:1],
                rim_smooth[:, 0:1],
            )
            for v, column in enumerate(columns):
                at = (sub + block * 8) * 4 + v
                total = jnp.where(lane == at, jnp.broadcast_to(column, (8, 128)), total)
        rim_own[pl.ds(plane, 1), :] = jnp.sum(total, axis=0, keepdims=True)

    pl.semaphore_wait(bar, LINES + 1)

    band_up = remote(rim_own, rim_bands.at[0], rim_sems.at[0, 0], rim_sems.at[1, 0], line, up)
    band_down = remote(rim_own, rim_bands.at[1], rim_sems.at[0, 1], rim_sems.at[1, 1], line, down)
    band_up.start()
    band_down.start()

    mine = held.at[pl.ds(pl.multiple_of(line * 16, 16), 16)]
    pltpu.make_async_copy(
        x_ref.at[pl.ds(pl.multiple_of(line * 16, 16), 16)], mine, arrive_sems.at[z // 4]
    ).start()

    def scatter(first, last):
        @pl.loop(first, last)
        def _(i):
            near = (i + 1) // 2
            to = wrap(line + jnp.where(i % 2 == 0, 64 - near, 64 + near), LINES)
            remote(
                x_ref.at[pl.ds(pl.multiple_of(to * 16, 16), 16)],
                mine,
                send_sem.at[0],
                arrive_sems.at[z // 4],
                to,
                tm,
            ).start()

    scatter(0, FIRST)

    band_up.wait_recv()
    band_down.wait_recv()
    lane16 = lax.broadcasted_iota(jnp.int32, (16, 128), 1)
    rim_merged[...] = jnp.where(lane16 % 4 < 2, rim_bands[0], rim_bands[1])
    for step in RING_STEPS:
        to = wrap(z + step, 16)
        remote(
            row_of(rim_merged, to),
            row_of(rim_ring, z),
            rim_sems.at[0, 3],
            rim_sems.at[1, 3],
            to * 8 + spot,
            tm,
        ).start()
    rim_ring[pl.ds(z, 1), :] = rim_merged[pl.ds(z, 1), :]

    scatter(FIRST, SECOND)

    settle(rim_ring.at[pl.ds(0, 15)], rim_sems.at[1, 3])
    for k in range(1, 8):
        remote(
            rim_ring,
            rim_plane.at[spot],
            rim_sems.at[0, 2],
            rim_sems.at[1, 2],
            z * 8 + wrap(spot + k, 8),
            tm,
        ).start()
    rim_plane[spot] = rim_ring[...]

    scatter(SECOND, LINES - 1)

    fetch_rates.wait()
    for group in range(GROUPS):
        total = jnp.zeros((8, 128), jnp.float32)
        for plane in range(PLANES):
            rate_row = rate_table[plane : plane + 1, :].astype(jnp.float32)
            picked = jnp.where(
                lane[:, :SHOTS] == sub[:, :SHOTS] + group * 8,
                jnp.broadcast_to(rate_row, (8, SHOTS)),
                0.0,
            )
            column = jnp.broadcast_to(jnp.sum(picked, axis=1, keepdims=True), (8, 128))
            rate_cols[plane, group * 8 : group * 8 + 8] = column
            total = total + column
        rate_cols[PLANES, group * 8 : group * 8 + 8] = total

    @pl.loop(0, SLOPE_ROWS)
    def _(row):
        kept_acc[row] = jnp.zeros((8, 128), jnp.float32)
        grid_index = (lane + row * 128).astype(jnp.float32)
        slope = jnp.exp2(slope_floor + grid_index * (slope_span / 2**BISECT))
        for plane in range(PLANES):
            for group in range(GROUPS):
                column = rate_cols[plane, group * 8 : group * 8 + 8]
                bars[row, plane, group * 8 : group * 8 + 8] = slope * column

    settle(rim_plane.at[pl.ds(0, 7)], rim_sems.at[1, 2])
    packed = jnp.zeros((16, 128), jnp.float32)
    for k in range(8):
        turned = pltpu.roll(rim_plane[k], lax.rem((k + 8 - spot) * 16, 128), 1)
        packed = jnp.where(lane16 // 16 == k, turned, packed)

    rims[pl.ds(0, 16, stride=2), :] = packed
    rims[pl.ds(1, 16, stride=2), :] = pltpu.roll(packed, 64, 1)

    has_prev_band = jnp.where(tm > 0, 1.0, 0.0)
    has_next_band = jnp.where(tm < BANDS - 1, 1.0, 0.0)
    has_prev_line = jnp.where(line > 0, 1.0, 0.0)
    has_next_line = jnp.where(line < LINES - 1, 1.0, 0.0)
    line_up = wrap(line + 1, LINES)
    line_down = wrap(line + LINES - 1, LINES)

    def line_copy(way, group):
        if way == 0:
            return remote(
                ahead_send.at[:, span(group)],
                ahead_recv.at[:, span(group)],
                line_sems.at[0, 0, group],
                line_sems.at[1, 0, group],
                line_down,
                tm,
            )
        return remote(
            back_send.at[:, span(group)],
            back_recv.at[:, span(group)],
            line_sems.at[0, 1, group],
            line_sems.at[1, 1, group],
            line_up,
            tm,
        )

    def group_at(turn):
        away = jnp.where(turn < 2, turn, 5 - turn)
        return wrap(z // 4 + away, GROUPS)

    @pl.loop(0, GROUPS)
    def _(turn):
        group = group_at(turn)
        settle(held.at[pl.ds(0, ROWS // GROUPS)], arrive_sems.at[group])
        rim = rims[span(group)]
        low = []
        high = []
        one = []
        three = []
        for r in range(16):
            at = 4 * r
            p0, p1, p2, p3 = [
                held[pl.ds(group * 512 + r * 4 + q, 8, stride=64), :] for q in range(4)
            ]
            d1 = detail(p0, p1, p2)
            ahead = jnp.where(
                lane == 127,
                pltpu.roll(rim, 125 - at, 1) * has_next_band,
                pltpu.roll(p0, 127, 1),
            )
            d3 = detail(p2, p3, ahead)
            rim_detail = pltpu.roll(rim, 128 - at, 1) if at else rim
            d3_prev = (rim_detail - 0.5 * p0) * has_prev_band
            s0 = smooth(p0, jnp.where(lane == 0, d3_prev, pltpu.roll(d3, 1, 1)), d1)
            s2 = smooth(p2, d1, d3)
            next_s0 = (pltpu.roll(rim, 124 - at, 1) + 0.25 * d3) * has_next_band
            second = detail(s0, s2, jnp.where(lane == 127, next_s0, pltpu.roll(s0, 127, 1)))
            rim_second = pltpu.roll(rim, 127 - at, 1)
            second_prev = (rim_second + 0.25 * d3_prev - 0.5 * s0) * has_prev_band
            first = smooth(
                s0, jnp.where(lane == 0, second_prev, pltpu.roll(second, 1, 1)), second
            )
            for slot, value in enumerate((s0, d1, s2, d3, first, second)):
                lifted[slot, r, span(group)] = value
            if r == 0:
                for slot, value in enumerate((s0, d1, s2, d3, first, second)):
                    ahead_send[slot, span(group)] = value
            one.append(d1)
            three.append(d3)
            low.append(first)
            high.append(second)
        for slot, value in enumerate((low, high)):
            ahead_send[6 + slot, span(group)] = value[0] + 0.25 * detail(value[0], value[1], value[2])
            d5 = detail(value[10], value[11], value[12])
            d6 = detail(value[12], value[13], value[14])
            s6 = smooth(value[12], d5, d6)
            back_send[4 + slot, span(group)] = value[14] + 0.25 * d6 - 0.5 * s6
        for slot, value in enumerate((one, three, low, high)):
            back_send[slot, span(group)] = value[15] - 0.5 * value[14]
        line_copy(0, group).start()
        line_copy(1, group).start()

    def put(group, r, q, value, gains):
        wave[pl.ds(group * 512 + r * 4 + q, 8, stride=64), :] = value
        square = value * value
        capped = [jnp.minimum(square, 4.0 ** (4 - p)) for p in range(PLANES + 1)]
        for p in range(PLANES):
            gains[p] = gains[p] + (capped[p] - capped[p + 1])

    @pl.loop(0, GROUPS)
    def _(turn):
        group = group_at(turn)
        gains = [jnp.zeros((8, 128), jnp.float32) for _ in range(PLANES)]
        for slot in range(6):
            values = [lifted[slot, r, span(group)] for r in range(15)]
            details = [
                detail(values[2 * i], values[2 * i + 1], values[2 * i + 2]) for i in range(7)
            ]
            if slot < 4:
                for i in range(7):
                    put(group, 2 * i + 1, slot, details[i], gains)
            if slot in (0, 2):
                continue
            smooths = [None] + [
                smooth(values[2 * i], details[i - 1], details[i]) for i in range(1, 7)
            ]
            if slot < 4:
                for i in range(1, 7):
                    put(group, 2 * i, slot, smooths[i], gains)
                continue
            second_one = detail(smooths[2], smooths[3], smooths[4])
            second_two = detail(smooths[4], smooths[5], smooths[6])
            q = (slot - 4) * 2
            put(group, 6, q, second_one, gains)
            put(group, 8, q, smooth(smooths[4], second_one, second_two), gains)
            put(group, 10, q, second_two, gains)
            kept_edges = (smooths[1], smooths[2], second_one, smooths[6], second_two)
            for n, value in enumerate(kept_edges):
                edges[slot - 4, n, span(group)] = value
        for p in range(PLANES):
            gain_acc[p, span(group)] = gains[p]

    @pl.loop(0, GROUPS)
    def _(turn):
        group = group_at(turn)
        line_copy(0, group).wait_recv()
        line_copy(1, group).wait_recv()
        gains = [gain_acc[p, span(group)] for p in range(PLANES)]
        for slot in range(6):
            first, early, third, before, odd, even, last = [
                lifted[slot, r, span(group)] for r in (0, 1, 2, 12, 13, 14, 15)
            ]
            ahead = ahead_recv[slot, span(group)] * has_next_line
            detail_last = detail(even, last, ahead)
            if slot < 4:
                put(group, 15, slot, detail_last, gains)
            if slot in (0, 2):
                continue
            back_slot = {1: 0, 3: 1, 4: 2, 5: 3}[slot]
            behind = (back_recv[back_slot, span(group)] - 0.5 * first) * has_prev_line
            smooth_first = smooth(first, behind, detail(first, early, third))
            smooth_last = smooth(even, detail(before, odd, even), detail_last)
            if slot < 4:
                put(group, 0, slot, smooth_first, gains)
                put(group, 14, slot, smooth_last, gains)
                continue
            k = slot - 4
            q = k * 2
            s1, s2, second_one, s6, second_two = [edges[k, n, span(group)] for n in range(5)]
            s8 = (ahead_recv[6 + k, span(group)] + 0.25 * detail_last) * has_next_line
            second_last = detail(s6, smooth_last, s8)
            second_first = detail(smooth_first, s1, s2)
            behind_two = (
                back_recv[4 + k, span(group)] + 0.25 * behind - 0.5 * smooth_first
            ) * has_prev_line
            put(group, 0, q, smooth(smooth_first, behind_two, second_first), gains)
            put(group, 2, q, second_first, gains)
            put(group, 4, q, smooth(s2, second_first, second_one), gains)
            put(group, 12, q, smooth(s6, second_two, second_last), gains)
            put(group, 14, q, second_last, gains)

        sums = [
            jnp.broadcast_to(jnp.sum(gains[p], axis=1, keepdims=True), (8, 128))
            for p in range(PLANES)
        ]
        rates = [rate_cols[p, span(group)] for p in range(PLANES)]

        @pl.loop(0, SLOPE_ROWS, unroll=4)
        def _(row):
            total = kept_acc[row]
            for p in range(PLANES):
                total = total + jnp.where(sums[p] >= bars[row, p, span(group)], rates[p], 0.0)
            kept_acc[row] = total

    out = pltpu.make_async_copy(wave, w_ref, own_sems.at[0])
    out.start()

    kept_rows[...] = jnp.sum(kept_acc[...], axis=1).astype(jnp.int32)
    place = plane_index(line, tm)

    for step in PLANE_STEPS:
        to_line, to_tm = plane_peer(step)
        remote(
            row_of(kept_rows, plane_index(to_line, to_tm)),
            row_of(plane_slots, place),
            tree_sems.at[0, 0],
            tree_sems.at[1, 0],
            to_line,
            to_tm,
        ).start()
    plane_slots[pl.ds(place, 1)] = kept_rows[pl.ds(place, 1)]
    settle(plane_slots.at[pl.ds(0, 31)], tree_sems.at[1, 0])
    ring_row[...] = jnp.sum(plane_slots[...], axis=0, keepdims=True)

    for step in RING_STEPS:
        remote(
            ring_row,
            row_of(ring_slots, z),
            tree_sems.at[0, 1],
            tree_sems.at[1, 1],
            wrap(line + step * 8, LINES),
            tm,
        ).start()
    ring_slots[pl.ds(z, 1)] = ring_row[...]
    settle(ring_slots.at[pl.ds(0, 15)], tree_sems.at[1, 1])
    kept = jnp.sum(ring_slots[...], axis=0, keepdims=True)
    limit = target_ref[0] * (SHOTS * LINES * BANDS)
    grid_row = lax.broadcasted_iota(jnp.int32, (1, 128), 1) + place * 128
    above = jnp.where((kept > limit) & (grid_row > 0), 1.0, 0.0)
    count_row[...] = jnp.broadcast_to(jnp.sum(above, axis=1, keepdims=True), (1, 128))

    for step in PLANE_STEPS:
        to_line, to_tm = plane_peer(step)
        remote(
            count_row,
            row_of(count_slots, place),
            tree_sems.at[0, 2],
            tree_sems.at[1, 2],
            to_line,
            to_tm,
        ).start()
    count_slots[pl.ds(place, 1)] = count_row[...]
    settle(count_slots.at[pl.ds(0, 31)], tree_sems.at[1, 2])
    chosen = 1.0 + jnp.sum(count_slots[...], axis=0, keepdims=True)
    slope_now = jnp.exp2(slope_floor + chosen * (slope_span / 2**BISECT))
    shrink_ref[...] = jnp.sqrt(slope_now * rate_cols[PLANES] / rate_scale)

    out.wait()
    settle(held.at[pl.ds(0, ROWS - 16)], send_sem.at[0])
    band_up.wait_send()
    band_down.wait_send()
    settle(rim_plane.at[pl.ds(0, 7)], rim_sems.at[0, 2])
    settle(rim_ring.at[pl.ds(0, 15)], rim_sems.at[0, 3])

    @pl.loop(0, GROUPS)
    def _(group):
        for way in range(2):
            line_copy(way, group).wait_send()

    settle(plane_slots.at[pl.ds(0, 31)], tree_sems.at[0, 0])
    settle(ring_slots.at[pl.ds(0, 15)], tree_sems.at[0, 1])
    settle(count_slots.at[pl.ds(0, 31)], tree_sems.at[0, 2])


def transform(rows, rates, byte_target):
    vmem = pl.BlockSpec(memory_space=pltpu.VMEM)
    hbm = pl.BlockSpec(memory_space=pl.ANY)
    rows, rates = [pltpu.with_memory_space_constraint(a, pltpu.HBM) for a in (rows, rates)]
    f32 = jnp.float32
    return pl.pallas_call(
        kernel,
        out_shape=[
            jax.ShapeDtypeStruct((ROWS, 128), f32),
            jax.ShapeDtypeStruct((SHOTS, 128), f32),
        ],
        in_specs=[hbm, hbm, pl.BlockSpec(memory_space=pltpu.SMEM)],
        out_specs=[hbm, vmem],
        scratch_shapes=[
            pltpu.VMEM((ROWS, 128), f32),
            pltpu.VMEM((ROWS, 128), f32),
            pltpu.VMEM((6, 16, SHOTS, 128), f32),
            pltpu.VMEM((ROWS, 128), f32),
            pltpu.VMEM((16, 128), f32),
            pltpu.VMEM((2, 16, 128), f32),
            pltpu.VMEM((16, 128), f32),
            pltpu.VMEM((8, 16, 128), f32),
            pltpu.VMEM((16, 128), f32),
            pltpu.VMEM((SHOTS, 128), f32),
            pltpu.VMEM((8, SHOTS, 128), f32),
            pltpu.VMEM((8, SHOTS, 128), f32),
            pltpu.VMEM((6, SHOTS, 128), f32),
            pltpu.VMEM((6, SHOTS, 128), f32),
            pltpu.VMEM((PLANES, SHOTS), jnp.int32),
            pltpu.VMEM((SLOPE_ROWS, PLANES, SHOTS, 128), f32),
            pltpu.VMEM((2, 5, SHOTS, 128), f32),
            pltpu.VMEM((PLANES, SHOTS, 128), f32),
            pltpu.VMEM((PLANES + 1, SHOTS, 128), f32),
            pltpu.VMEM((SLOPE_ROWS, 8, 128), f32),
            pltpu.VMEM((SLOPE_ROWS, 128), jnp.int32),
            pltpu.VMEM((SLOPE_ROWS, 128), jnp.int32),
            pltpu.VMEM((1, 128), jnp.int32),
            pltpu.VMEM((16, 128), jnp.int32),
            pltpu.VMEM((1, 128), f32),
            pltpu.VMEM((32, 128), f32),
            pltpu.SemaphoreType.DMA((2,)),
            pltpu.SemaphoreType.DMA((1,)),
            pltpu.SemaphoreType.DMA((GROUPS,)),
            pltpu.SemaphoreType.DMA((2, 4)),
            pltpu.SemaphoreType.DMA((2, 2, GROUPS)),
            pltpu.SemaphoreType.DMA((2, 3)),
        ],
        compiler_params=pltpu.CompilerParams(
            collective_id=1, has_side_effects=True, vmem_limit_bytes=24 * 2**20
        ),
        name="transform",
    )(rows, rates, byte_target)


def body(traces, rates, byte_target):
    width = traces.shape[3]
    rows = traces.reshape(ROWS, width)
    wave, shrink = transform(rows, rates.reshape(PLANES, SHOTS), byte_target)
    wavelet = wave.reshape(SHOTS, 16, 4, width)
    shrink_by = shrink[:, None, None, :]
    return wavelet - jnp.clip(wavelet, -shrink_by, shrink_by)


def solution(mesh):
    return jax.shard_map(
        body,
        mesh=mesh,
        in_specs=(P("line", None, None, "tm"), P("line", "tm", None, None), P()),
        out_specs=P(None, "line", None, "tm"),
        check_vma=False,
    )
```

```python
import jax
import jax.numpy as jnp
from jax import lax
from jax.experimental import pallas as pl
from jax.experimental.pallas import tpu as pltpu
from jax.sharding import PartitionSpec as P

PLANES = 8
BISECT = 12
LINES = 128
BANDS = 4
SHOTS = 32
GROUPS = 4
ROWS = 2048
FIRST = 32
SECOND = 112
SLOPE_ROWS = 2**BISECT // 128
MESH = pl.DeviceIdType.MESH

slope_floor = -12.0
slope_span = 32.0
rate_scale = 65536.0

PLANE_STEPS = sorted(
    [(dx, dy) for dx in range(4) for dy in range(4)][1:],
    key=lambda s: (-(min(s[0], 4 - s[0]) + min(s[1], 4 - s[1])), s),
)
RING_STEPS = sorted(range(1, 16), key=lambda s: -min(s, 16 - s))


def remote(src, dst, ssem, rsem, line, tm):
    return pltpu.make_async_remote_copy(
        src_ref=src,
        dst_ref=dst,
        send_sem=ssem,
        recv_sem=rsem,
        device_id=(line, tm),
        device_id_type=MESH,
    )


def settle(ref, sem):
    pltpu.make_async_copy(ref, ref, sem).wait()


def wrap(value, count):
    return jnp.where(value >= count, value - count, value)


def detail(even_part, odd_part, ahead_even):
    return odd_part - 0.5 * (even_part + ahead_even)


def smooth(even_part, behind, details):
    return even_part + 0.25 * (behind + details)


def kernel(
    x_ref,
    rates_ref,
    target_ref,
    w_ref,
    shrink_ref,
    local,
    held,
    lifted,
    wave,
    rim_own,
    rim_bands,
    rim_merged,
    rim_plane,
    rim_ring,
    rims,
    ahead_send,
    ahead_recv,
    back_send,
    back_recv,
    rate_table,
    bars,
    edges,
    gain_acc,
    rate_cols,
    kept_acc,
    kept_rows,
    plane_slots,
    ring_row,
    ring_slots,
    count_row,
    count_slots,
    own_sems,
    send_sem,
    arrive_sems,
    rim_sems,
    line_sems,
    tree_sems,
):
    line = lax.axis_index("line")
    tm = lax.axis_index("tm")
    z = line // 8
    x = (line // 2) % 4
    core = line % 2
    spot = line % 8

    peer_place = [wrap(x + k, 4) * 4 for k in range(4)]
    peer_x = [(z * 4 + wrap(x + k, 4)) * 2 for k in range(4)]
    peer_tm = [wrap(tm + k, 4) for k in range(4)]

    def plane_peer(step):
        dx, dy = step
        return peer_x[dx] + core, peer_tm[dy], peer_place[dx] + peer_tm[dy]

    def span(group):
        return pl.ds(pl.multiple_of(group * 8, 8), 8)

    def row_of(ref, index):
        return ref.at[pl.ds(index, 1)]

    fetch = pltpu.make_async_copy(x_ref, local.at[pl.ds(0, ROWS)], own_sems.at[0])
    fetch.start()
    fetch_rates = pltpu.make_async_copy(rates_ref, rate_table, own_sems.at[1])
    fetch_rates.start()

    up, down = peer_tm[1], peer_tm[3]
    bar = pltpu.get_barrier_semaphore()

    @pl.loop(0, 15)
    def _(i):
        near = 8 - (i + 1) // 2
        step = jnp.where(i % 2 == 0, near, 16 - near)
        plane = wrap(z + step, 16) * 8
        for k in range(8):
            pl.semaphore_signal(bar, inc=1, device_id=(plane + k, tm), device_id_type=MESH)

    for k in range(1, 8):
        pl.semaphore_signal(
            bar, inc=1, device_id=(z * 8 + wrap(spot + k, 8), tm), device_id_type=MESH
        )
    for to in (up, down):
        pl.semaphore_signal(bar, inc=1, device_id=(line, to), device_id_type=MESH)

    lane = lax.broadcasted_iota(jnp.int32, (8, 128), 1)
    sub = lax.broadcasted_iota(jnp.int32, (8, 128), 0)
    fetch.wait()

    @pl.loop(0, 16)
    def _(plane):
        total = jnp.zeros((8, 128), jnp.float32)
        for block in range(4):
            p0, p1, p2, p3 = [
                local[pl.ds(plane * 128 + block * 32 + q, 8, stride=4), :] for q in range(4)
            ]
            d1 = detail(p0, p1, p2)
            d3 = detail(p2, p3, pltpu.roll(p0, 127, 1))
            s0 = smooth(p0, pltpu.roll(d3, 1, 1), d1)
            rim_detail = p3 - 0.5 * p2
            rim_second = p2 + 0.25 * d1 - 0.5 * s0
            rim_smooth = p0 + 0.25 * d1
            columns = (
                rim_detail[:, 127:128],
                rim_second[:, 127:128],
                p0[:, 0:1],
                rim_smooth[:, 0:1],
            )
            for v, column in enumerate(columns):
                at = (sub + block * 8) * 4 + v
                total = jnp.where(lane == at, jnp.broadcast_to(column, (8, 128)), total)
        rim_own[pl.ds(plane, 1), :] = jnp.sum(total, axis=0, keepdims=True)

    pl.semaphore_wait(bar, LINES + 1)

    band_up = remote(rim_own, rim_bands.at[0], rim_sems.at[0, 0], rim_sems.at[1, 0], line, up)
    band_down = remote(rim_own, rim_bands.at[1], rim_sems.at[0, 1], rim_sems.at[1, 1], line, down)
    band_up.start()
    band_down.start()

    mine = held.at[pl.ds(pl.multiple_of(line * 16, 16), 16)]
    pltpu.make_async_copy(
        x_ref.at[pl.ds(pl.multiple_of(line * 16, 16), 16)], mine, arrive_sems.at[z // 4]
    ).start()

    def scatter(first, last):
        @pl.loop(first, last)
        def _(i):
            near = (i + 1) // 2
            to = wrap(line + jnp.where(i % 2 == 0, 64 - near, 64 + near), LINES)
            remote(
                x_ref.at[pl.ds(pl.multiple_of(to * 16, 16), 16)],
                mine,
                send_sem.at[0],
                arrive_sems.at[z // 4],
                to,
                tm,
            ).start()

    scatter(0, FIRST)

    band_up.wait_recv()
    band_down.wait_recv()
    lane16 = lax.broadcasted_iota(jnp.int32, (16, 128), 1)
    rim_merged[...] = jnp.where(lane16 % 4 < 2, rim_bands[0], rim_bands[1])
    for step in RING_STEPS:
        to = wrap(z + step, 16)
        remote(
            row_of(rim_merged, to),
            row_of(rim_ring, z),
            rim_sems.at[0, 3],
            rim_sems.at[1, 3],
            to * 8 + spot,
            tm,
        ).start()
    rim_ring[pl.ds(z, 1), :] = rim_merged[pl.ds(z, 1), :]

    scatter(FIRST, SECOND)

    settle(rim_ring.at[pl.ds(0, 15)], rim_sems.at[1, 3])
    for k in range(1, 8):
        remote(
            rim_ring,
            rim_plane.at[spot],
            rim_sems.at[0, 2],
            rim_sems.at[1, 2],
            z * 8 + wrap(spot + k, 8),
            tm,
        ).start()
    rim_plane[spot] = rim_ring[...]

    scatter(SECOND, LINES - 1)

    fetch_rates.wait()
    for group in range(GROUPS):
        total = jnp.zeros((8, 128), jnp.float32)
        for plane in range(PLANES):
            rate_row = rate_table[plane : plane + 1, :].astype(jnp.float32)
            picked = jnp.where(
                lane[:, :SHOTS] == sub[:, :SHOTS] + group * 8,
                jnp.broadcast_to(rate_row, (8, SHOTS)),
                0.0,
            )
            column = jnp.broadcast_to(jnp.sum(picked, axis=1, keepdims=True), (8, 128))
            rate_cols[plane, group * 8 : group * 8 + 8] = column
            total = total + column
        rate_cols[PLANES, group * 8 : group * 8 + 8] = total

    @pl.loop(0, SLOPE_ROWS)
    def _(row):
        kept_acc[row] = jnp.zeros((8, 128), jnp.float32)
        grid_index = (lane + row * 128).astype(jnp.float32)
        slope = jnp.exp2(slope_floor + grid_index * (slope_span / 2**BISECT))
        for plane in range(PLANES):
            for group in range(GROUPS):
                column = rate_cols[plane, group * 8 : group * 8 + 8]
                bars[row, plane, group * 8 : group * 8 + 8] = slope * column

    settle(rim_plane.at[pl.ds(0, 7)], rim_sems.at[1, 2])
    packed = jnp.zeros((16, 128), jnp.float32)
    for k in range(8):
        turned = pltpu.roll(rim_plane[k], lax.rem((k + 8 - spot) * 16, 128), 1)
        packed = jnp.where(lane16 // 16 == k, turned, packed)

    rims[pl.ds(0, 16, stride=2), :] = packed
    rims[pl.ds(1, 16, stride=2), :] = pltpu.roll(packed, 64, 1)

    has_prev_band = jnp.where(tm > 0, 1.0, 0.0)
    has_next_band = jnp.where(tm < BANDS - 1, 1.0, 0.0)
    has_prev_line = jnp.where(line > 0, 1.0, 0.0)
    has_next_line = jnp.where(line < LINES - 1, 1.0, 0.0)
    line_up = wrap(line + 1, LINES)
    line_down = wrap(line + LINES - 1, LINES)

    def line_copy(way, group):
        if way == 0:
            return remote(
                ahead_send.at[:, span(group)],
                ahead_recv.at[:, span(group)],
                line_sems.at[0, 0, group],
                line_sems.at[1, 0, group],
                line_down,
                tm,
            )
        return remote(
            back_send.at[:, span(group)],
            back_recv.at[:, span(group)],
            line_sems.at[0, 1, group],
            line_sems.at[1, 1, group],
            line_up,
            tm,
        )

    def group_at(turn):
        away = jnp.where(turn < 2, turn, 5 - turn)
        return wrap(z // 4 + away, GROUPS)

    def lift_time(group, rim, r):
        at = 4 * r
        p0, p1, p2, p3 = [
            held[pl.ds(group * 512 + r * 4 + q, 8, stride=64), :] for q in range(4)
        ]
        d1 = detail(p0, p1, p2)
        ahead = jnp.where(
            lane == 127,
            pltpu.roll(rim, 125 - at, 1) * has_next_band,
            pltpu.roll(p0, 127, 1),
        )
        d3 = detail(p2, p3, ahead)
        rim_detail = pltpu.roll(rim, 128 - at, 1) if at else rim
        d3_prev = (rim_detail - 0.5 * p0) * has_prev_band
        s0 = smooth(p0, jnp.where(lane == 0, d3_prev, pltpu.roll(d3, 1, 1)), d1)
        s2 = smooth(p2, d1, d3)
        next_s0 = (pltpu.roll(rim, 124 - at, 1) + 0.25 * d3) * has_next_band
        second = detail(s0, s2, jnp.where(lane == 127, next_s0, pltpu.roll(s0, 127, 1)))
        rim_second = pltpu.roll(rim, 127 - at, 1)
        second_prev = (rim_second + 0.25 * d3_prev - 0.5 * s0) * has_prev_band
        first = smooth(
            s0, jnp.where(lane == 0, second_prev, pltpu.roll(second, 1, 1)), second
        )
        values = (s0, d1, s2, d3, first, second)
        for slot, value in enumerate(values):
            lifted[slot, r, span(group)] = value
        return values

    @pl.loop(0, GROUPS)
    def _(turn):
        group = group_at(turn)
        settle(held.at[pl.ds(0, ROWS // GROUPS)], arrive_sems.at[group])
        rim = rims[span(group)]
        ends = {r: lift_time(group, rim, r) for r in (0, 1, 2, 10, 11, 12, 13, 14, 15)}
        for slot, value in enumerate(ends[0]):
            ahead_send[slot, span(group)] = value
        for slot, plane in enumerate((4, 5)):
            value = {r: values[plane] for r, values in ends.items()}
            ahead_send[6 + slot, span(group)] = value[0] + 0.25 * detail(value[0], value[1], value[2])
            d5 = detail(value[10], value[11], value[12])
            d6 = detail(value[12], value[13], value[14])
            s6 = smooth(value[12], d5, d6)
            back_send[4 + slot, span(group)] = value[14] + 0.25 * d6 - 0.5 * s6
        for slot, plane in enumerate((1, 3, 4, 5)):
            back_send[slot, span(group)] = ends[15][plane] - 0.5 * ends[14][plane]
        line_copy(0, group).start()
        line_copy(1, group).start()

    @pl.loop(0, GROUPS)
    def _(turn):
        group = group_at(turn)
        rim = rims[span(group)]
        for r in range(3, 10):
            lift_time(group, rim, r)

    def put(group, r, q, value, gains):
        wave[pl.ds(group * 512 + r * 4 + q, 8, stride=64), :] = value
        square = value * value
        capped = [jnp.minimum(square, 4.0 ** (4 - p)) for p in range(PLANES + 1)]
        for p in range(PLANES):
            gains[p] = gains[p] + (capped[p] - capped[p + 1])

    @pl.loop(0, GROUPS)
    def _(turn):
        group = group_at(turn)
        gains = [jnp.zeros((8, 128), jnp.float32) for _ in range(PLANES)]
        for slot in range(6):
            values = [lifted[slot, r, span(group)] for r in range(15)]
            details = [
                detail(values[2 * i], values[2 * i + 1], values[2 * i + 2]) for i in range(7)
            ]
            if slot < 4:
                for i in range(7):
                    put(group, 2 * i + 1, slot, details[i], gains)
            if slot in (0, 2):
                continue
            smooths = [None] + [
                smooth(values[2 * i], details[i - 1], details[i]) for i in range(1, 7)
            ]
            if slot < 4:
                for i in range(1, 7):
                    put(group, 2 * i, slot, smooths[i], gains)
                continue
            second_one = detail(smooths[2], smooths[3], smooths[4])
            second_two = detail(smooths[4], smooths[5], smooths[6])
            q = (slot - 4) * 2
            put(group, 6, q, second_one, gains)
            put(group, 8, q, smooth(smooths[4], second_one, second_two), gains)
            put(group, 10, q, second_two, gains)
            kept_edges = (smooths[1], smooths[2], second_one, smooths[6], second_two)
            for n, value in enumerate(kept_edges):
                edges[slot - 4, n, span(group)] = value
        for p in range(PLANES):
            gain_acc[p, span(group)] = gains[p]

    @pl.loop(0, GROUPS)
    def _(turn):
        group = group_at(turn)
        line_copy(0, group).wait_recv()
        line_copy(1, group).wait_recv()
        gains = [gain_acc[p, span(group)] for p in range(PLANES)]
        for slot in range(6):
            first, early, third, before, odd, even, last = [
                lifted[slot, r, span(group)] for r in (0, 1, 2, 12, 13, 14, 15)
            ]
            ahead = ahead_recv[slot, span(group)] * has_next_line
            detail_last = detail(even, last, ahead)
            if slot < 4:
                put(group, 15, slot, detail_last, gains)
            if slot in (0, 2):
                continue
            back_slot = {1: 0, 3: 1, 4: 2, 5: 3}[slot]
            behind = (back_recv[back_slot, span(group)] - 0.5 * first) * has_prev_line
            smooth_first = smooth(first, behind, detail(first, early, third))
            smooth_last = smooth(even, detail(before, odd, even), detail_last)
            if slot < 4:
                put(group, 0, slot, smooth_first, gains)
                put(group, 14, slot, smooth_last, gains)
                continue
            k = slot - 4
            q = k * 2
            s1, s2, second_one, s6, second_two = [edges[k, n, span(group)] for n in range(5)]
            s8 = (ahead_recv[6 + k, span(group)] + 0.25 * detail_last) * has_next_line
            second_last = detail(s6, smooth_last, s8)
            second_first = detail(smooth_first, s1, s2)
            behind_two = (
                back_recv[4 + k, span(group)] + 0.25 * behind - 0.5 * smooth_first
            ) * has_prev_line
            put(group, 0, q, smooth(smooth_first, behind_two, second_first), gains)
            put(group, 2, q, second_first, gains)
            put(group, 4, q, smooth(s2, second_first, second_one), gains)
            put(group, 12, q, smooth(s6, second_two, second_last), gains)
            put(group, 14, q, second_last, gains)

        sums = [
            jnp.broadcast_to(jnp.sum(gains[p], axis=1, keepdims=True), (8, 128))
            for p in range(PLANES)
        ]
        rates = [rate_cols[p, span(group)] for p in range(PLANES)]

        @pl.loop(0, SLOPE_ROWS, unroll=4)
        def _(row):
            total = kept_acc[row]
            for p in range(PLANES):
                total = total + jnp.where(sums[p] >= bars[row, p, span(group)], rates[p], 0.0)
            kept_acc[row] = total

    out = pltpu.make_async_copy(wave.at[pl.ds(0, ROWS)], w_ref, own_sems.at[0])
    out.start()

    half = SLOPE_ROWS // 2
    kept_rows[:, 0:128] = jnp.sum(kept_acc[0:half], axis=1).astype(jnp.int32)
    kept_rows[:, 128:256] = jnp.sum(kept_acc[half:SLOPE_ROWS], axis=1).astype(jnp.int32)
    place = peer_place[0] + tm

    for step in PLANE_STEPS:
        to_line, to_tm, to_place = plane_peer(step)
        remote(
            row_of(kept_rows, to_place),
            row_of(plane_slots, place),
            tree_sems.at[0, 0],
            tree_sems.at[1, 0],
            to_line,
            to_tm,
        ).start()
    plane_slots[pl.ds(place, 1)] = kept_rows[pl.ds(place, 1)]
    settle(held.at[pl.ds(0, 30)], tree_sems.at[1, 0])
    ring_row[...] = jnp.sum(plane_slots[...], axis=0, keepdims=True)

    for step in RING_STEPS + [0]:
        plane = wrap(z + step, 16) * 8 + spot
        for to in (plane, plane + 1 - 2 * core):
            if step == 0 and to is plane:
                continue
            remote(
                ring_row,
                row_of(ring_slots, z * 2 + core),
                tree_sems.at[0, 1],
                tree_sems.at[1, 1],
                to,
                tm,
            ).start()
    ring_slots[pl.ds(z * 2 + core, 1)] = ring_row[...]
    settle(held.at[pl.ds(0, 62)], tree_sems.at[1, 1])
    kept = jnp.sum(ring_slots[...], axis=0, keepdims=True)
    limit = target_ref[0] * (SHOTS * LINES * BANDS)
    lane256 = lax.broadcasted_iota(jnp.int32, (1, 256), 1)
    grid_row = place * 128 + jnp.where(lane256 < 128, lane256, lane256 + 2**BISECT // 2 - 128)
    above = jnp.where((kept > limit) & (grid_row > 0), 1.0, 0.0)
    count_row[...] = jnp.broadcast_to(jnp.sum(above, axis=1, keepdims=True), (1, 128))

    for step in PLANE_STEPS:
        to_line, to_tm, _ = plane_peer(step)
        remote(
            count_row,
            row_of(count_slots, place),
            tree_sems.at[0, 2],
            tree_sems.at[1, 2],
            to_line,
            to_tm,
        ).start()
    count_slots[pl.ds(place, 1)] = count_row[...]
    settle(count_slots.at[pl.ds(0, 15)], tree_sems.at[1, 2])
    chosen = 1.0 + jnp.sum(count_slots[...], axis=0, keepdims=True)
    slope_now = jnp.exp2(slope_floor + chosen * (slope_span / 2**BISECT))
    shrink_ref[...] = jnp.sqrt(slope_now * rate_cols[PLANES] / rate_scale)

    out.wait()
    settle(held.at[pl.ds(0, ROWS - 16)], send_sem.at[0])
    band_up.wait_send()
    band_down.wait_send()
    settle(rim_plane.at[pl.ds(0, 7)], rim_sems.at[0, 2])
    settle(rim_ring.at[pl.ds(0, 15)], rim_sems.at[0, 3])

    @pl.loop(0, GROUPS)
    def _(group):
        for way in range(2):
            line_copy(way, group).wait_send()

    settle(held.at[pl.ds(0, 30)], tree_sems.at[0, 0])
    settle(held.at[pl.ds(0, 62)], tree_sems.at[0, 1])
    settle(count_slots.at[pl.ds(0, 15)], tree_sems.at[0, 2])


def transform(rows, rates, byte_target):
    vmem = pl.BlockSpec(memory_space=pltpu.VMEM)
    hbm = pl.BlockSpec(memory_space=pl.ANY)
    rows, rates = [pltpu.with_memory_space_constraint(a, pltpu.HBM) for a in (rows, rates)]
    f32 = jnp.float32
    return pl.pallas_call(
        kernel,
        out_shape=[
            jax.ShapeDtypeStruct((ROWS, 128), f32),
            jax.ShapeDtypeStruct((SHOTS, 128), f32),
        ],
        in_specs=[hbm, hbm, pl.BlockSpec(memory_space=pltpu.SMEM)],
        out_specs=[hbm, vmem],
        scratch_shapes=[
            pltpu.VMEM((ROWS + 64, 128), f32),
            pltpu.VMEM((ROWS + 64, 128), f32),
            pltpu.VMEM((6, 16, SHOTS, 128), f32),
            pltpu.VMEM((ROWS + 64, 128), f32),
            pltpu.VMEM((16, 128), f32),
            pltpu.VMEM((2, 16, 128), f32),
            pltpu.VMEM((16, 128), f32),
            pltpu.VMEM((8, 16, 128), f32),
            pltpu.VMEM((16, 128), f32),
            pltpu.VMEM((SHOTS + 8, 128), f32),
            pltpu.VMEM((8, SHOTS, 128), f32),
            pltpu.VMEM((8, SHOTS, 128), f32),
            pltpu.VMEM((6, SHOTS, 128), f32),
            pltpu.VMEM((6, SHOTS, 128), f32),
            pltpu.VMEM((PLANES, SHOTS), jnp.int32),
            pltpu.VMEM((SLOPE_ROWS, PLANES, SHOTS, 128), f32),
            pltpu.VMEM((2, 5, SHOTS, 128), f32),
            pltpu.VMEM((PLANES, SHOTS, 128), f32),
            pltpu.VMEM((PLANES + 1, SHOTS, 128), f32),
            pltpu.VMEM((SLOPE_ROWS, 8, 128), f32),
            pltpu.VMEM((16, 256), jnp.int32),
            pltpu.VMEM((16, 256), jnp.int32),
            pltpu.VMEM((1, 256), jnp.int32),
            pltpu.VMEM((32, 256), jnp.int32),
            pltpu.VMEM((1, 128), f32),
            pltpu.VMEM((16, 128), f32),
            pltpu.SemaphoreType.DMA((2,)),
            pltpu.SemaphoreType.DMA((1,)),
            pltpu.SemaphoreType.DMA((GROUPS,)),
            pltpu.SemaphoreType.DMA((2, 4)),
            pltpu.SemaphoreType.DMA((2, 2, GROUPS)),
            pltpu.SemaphoreType.DMA((2, 3)),
        ],
        compiler_params=pltpu.CompilerParams(
            collective_id=1, has_side_effects=True, vmem_limit_bytes=24 * 2**20
        ),
        name="transform",
    )(rows, rates, byte_target)


def body(traces, rates, byte_target):
    width = traces.shape[3]
    rows = traces.reshape(ROWS, width)
    wave, shrink = transform(rows, rates.reshape(PLANES, SHOTS), byte_target)
    wavelet = wave.reshape(SHOTS, 16, 4, width)
    shrink_by = shrink[:, None, None, :]
    return wavelet - jnp.clip(wavelet, -shrink_by, shrink_by)


def solution(mesh):
    return jax.shard_map(
        body,
        mesh=mesh,
        in_specs=(P("line", None, None, "tm"), P("line", "tm", None, None), P()),
        out_specs=P(None, "line", None, "tm"),
        check_vma=False,
    )
```

```python
import jax
import jax.numpy as jnp
from jax import lax
from jax.experimental import pallas as pl
from jax.experimental.pallas import tpu as pltpu
from jax.sharding import PartitionSpec as P

PLANES = 8
BISECT = 12
LINES = 128
BANDS = 4
SHOTS = 32
GROUPS = 4
ROWS = 2048
CHUNKS = 8
FIRST = 32
SECOND = 112
SLOPE_ROWS = 2**BISECT // 128
MESH = pl.DeviceIdType.MESH

slope_floor = -12.0
slope_span = 32.0
rate_scale = 65536.0

PLANE_STEPS = sorted(
    [(dx, dy) for dx in range(4) for dy in range(4)][1:],
    key=lambda s: (-(min(s[0], 4 - s[0]) + min(s[1], 4 - s[1])), s),
)
RING_STEPS = sorted(range(1, 16), key=lambda s: -min(s, 16 - s))


def remote(src, dst, ssem, rsem, line, tm):
    return pltpu.make_async_remote_copy(
        src_ref=src,
        dst_ref=dst,
        send_sem=ssem,
        recv_sem=rsem,
        device_id=(line, tm),
        device_id_type=MESH,
    )


def settle(ref, sem):
    pltpu.make_async_copy(ref, ref, sem).wait()


def wrap(value, count):
    return jnp.where(value >= count, value - count, value)


def detail(even_part, odd_part, ahead_even):
    return odd_part - 0.5 * (even_part + ahead_even)


def smooth(even_part, behind, details):
    return even_part + 0.25 * (behind + details)


def kernel(
    x_ref,
    rates_ref,
    target_ref,
    w_ref,
    shrink_ref,
    local,
    held,
    lifted,
    wave,
    rim_own,
    rim_bands,
    rim_merged,
    rim_plane,
    rim_ring,
    rims,
    ahead_send,
    ahead_recv,
    back_send,
    back_recv,
    rate_table,
    bars,
    edges,
    gain_acc,
    rate_cols,
    kept_acc,
    kept_rows,
    plane_slots,
    ring_row,
    ring_slots,
    count_row,
    count_slots,
    own_sems,
    send_sem,
    arrive_sems,
    rim_sems,
    line_sems,
    tree_sems,
):
    line = lax.axis_index("line")
    tm = lax.axis_index("tm")
    z = line // 8
    x = (line // 2) % 4
    core = line % 2
    spot = line % 8

    peer_place = [wrap(x + k, 4) * 4 for k in range(4)]
    peer_x = [(z * 4 + wrap(x + k, 4)) * 2 for k in range(4)]
    peer_tm = [wrap(tm + k, 4) for k in range(4)]

    def plane_peer(step):
        dx, dy = step
        return peer_x[dx] + core, peer_tm[dy], peer_place[dx] + peer_tm[dy]

    def span(group):
        return pl.ds(pl.multiple_of(group * 8, 8), 8)

    def row_of(ref, index):
        return ref.at[pl.ds(index, 1)]

    fetch = pltpu.make_async_copy(x_ref, local.at[pl.ds(0, ROWS)], own_sems.at[0])
    fetch.start()
    fetch_rates = pltpu.make_async_copy(rates_ref, rate_table, own_sems.at[1])
    fetch_rates.start()

    up, down = peer_tm[1], peer_tm[3]
    bar = pltpu.get_barrier_semaphore()

    @pl.loop(0, 15)
    def _(i):
        near = 8 - (i + 1) // 2
        step = jnp.where(i % 2 == 0, near, 16 - near)
        plane = wrap(z + step, 16) * 8
        for k in range(8):
            pl.semaphore_signal(bar, inc=1, device_id=(plane + k, tm), device_id_type=MESH)

    for k in range(1, 8):
        pl.semaphore_signal(
            bar, inc=1, device_id=(z * 8 + wrap(spot + k, 8), tm), device_id_type=MESH
        )
    for to in (up, down):
        pl.semaphore_signal(bar, inc=1, device_id=(line, to), device_id_type=MESH)

    lane = lax.broadcasted_iota(jnp.int32, (8, 128), 1)
    sub = lax.broadcasted_iota(jnp.int32, (8, 128), 0)
    fetch.wait()

    @pl.loop(0, 16)
    def _(plane):
        total = jnp.zeros((8, 128), jnp.float32)
        for block in range(4):
            p0, p1, p2, p3 = [
                local[pl.ds(plane * 128 + block * 32 + q, 8, stride=4), :] for q in range(4)
            ]
            d1 = detail(p0, p1, p2)
            d3 = detail(p2, p3, pltpu.roll(p0, 127, 1))
            s0 = smooth(p0, pltpu.roll(d3, 1, 1), d1)
            rim_detail = p3 - 0.5 * p2
            rim_second = p2 + 0.25 * d1 - 0.5 * s0
            rim_smooth = p0 + 0.25 * d1
            columns = (
                rim_detail[:, 127:128],
                rim_second[:, 127:128],
                p0[:, 0:1],
                rim_smooth[:, 0:1],
            )
            for v, column in enumerate(columns):
                at = (sub + block * 8) * 4 + v
                total = jnp.where(lane == at, jnp.broadcast_to(column, (8, 128)), total)
        rim_own[pl.ds(plane, 1), :] = jnp.sum(total, axis=0, keepdims=True)

    pl.semaphore_wait(bar, LINES + 1)

    band_up = remote(rim_own, rim_bands.at[0], rim_sems.at[0, 0], rim_sems.at[1, 0], line, up)
    band_down = remote(rim_own, rim_bands.at[1], rim_sems.at[0, 1], rim_sems.at[1, 1], line, down)
    band_up.start()
    band_down.start()

    mine = held.at[pl.ds(pl.multiple_of(line * 16, 16), 16)]
    pltpu.make_async_copy(
        x_ref.at[pl.ds(pl.multiple_of(line * 16, 16), 16)], mine, arrive_sems.at[z // 4]
    ).start()

    def scatter(first, last):
        @pl.loop(first, last)
        def _(i):
            near = (i + 1) // 2
            to = wrap(line + jnp.where(i % 2 == 0, 64 - near, 64 + near), LINES)
            remote(
                x_ref.at[pl.ds(pl.multiple_of(to * 16, 16), 16)],
                mine,
                send_sem.at[0],
                arrive_sems.at[z // 4],
                to,
                tm,
            ).start()

    scatter(0, FIRST)

    band_up.wait_recv()
    band_down.wait_recv()
    lane16 = lax.broadcasted_iota(jnp.int32, (16, 128), 1)
    rim_merged[...] = jnp.where(lane16 % 4 < 2, rim_bands[0], rim_bands[1])
    for step in RING_STEPS:
        to = wrap(z + step, 16)
        remote(
            row_of(rim_merged, to),
            row_of(rim_ring, z),
            rim_sems.at[0, 3],
            rim_sems.at[1, 3],
            to * 8 + spot,
            tm,
        ).start()
    rim_ring[pl.ds(z, 1), :] = rim_merged[pl.ds(z, 1), :]

    scatter(FIRST, SECOND)

    settle(rim_ring.at[pl.ds(0, 15)], rim_sems.at[1, 3])
    for k in range(1, 8):
        remote(
            rim_ring,
            rim_plane.at[spot],
            rim_sems.at[0, 2],
            rim_sems.at[1, 2],
            z * 8 + wrap(spot + k, 8),
            tm,
        ).start()
    rim_plane[spot] = rim_ring[...]

    scatter(SECOND, LINES - 1)

    fetch_rates.wait()
    for group in range(GROUPS):
        total = jnp.zeros((8, 128), jnp.float32)
        for plane in range(PLANES):
            rate_row = rate_table[plane : plane + 1, :].astype(jnp.float32)
            picked = jnp.where(
                lane[:, :SHOTS] == sub[:, :SHOTS] + group * 8,
                jnp.broadcast_to(rate_row, (8, SHOTS)),
                0.0,
            )
            column = jnp.broadcast_to(jnp.sum(picked, axis=1, keepdims=True), (8, 128))
            rate_cols[plane, group * 8 : group * 8 + 8] = column
            total = total + column
        rate_cols[PLANES, group * 8 : group * 8 + 8] = total

    @pl.loop(0, SLOPE_ROWS)
    def _(row):
        kept_acc[row] = jnp.zeros((8, 128), jnp.float32)
        grid_index = (lane + row * 128).astype(jnp.float32)
        slope = jnp.exp2(slope_floor + grid_index * (slope_span / 2**BISECT))
        for plane in range(PLANES):
            for group in range(GROUPS):
                column = rate_cols[plane, group * 8 : group * 8 + 8]
                bars[row, plane, group * 8 : group * 8 + 8] = slope * column

    settle(rim_plane.at[pl.ds(0, 7)], rim_sems.at[1, 2])
    packed = jnp.zeros((16, 128), jnp.float32)
    for k in range(8):
        turned = pltpu.roll(rim_plane[k], lax.rem((k + 8 - spot) * 16, 128), 1)
        packed = jnp.where(lane16 // 16 == k, turned, packed)

    rims[pl.ds(0, 16, stride=2), :] = packed
    rims[pl.ds(1, 16, stride=2), :] = pltpu.roll(packed, 64, 1)

    has_prev_band = jnp.where(tm > 0, 1.0, 0.0)
    has_next_band = jnp.where(tm < BANDS - 1, 1.0, 0.0)
    has_prev_line = jnp.where(line > 0, 1.0, 0.0)
    has_next_line = jnp.where(line < LINES - 1, 1.0, 0.0)
    line_up = wrap(line + 1, LINES)
    line_down = wrap(line + LINES - 1, LINES)

    def line_copy(way, group):
        if way == 0:
            return remote(
                ahead_send.at[:, span(group)],
                ahead_recv.at[:, span(group)],
                line_sems.at[0, 0, group],
                line_sems.at[1, 0, group],
                line_down,
                tm,
            )
        return remote(
            back_send.at[:, span(group)],
            back_recv.at[:, span(group)],
            line_sems.at[0, 1, group],
            line_sems.at[1, 1, group],
            line_up,
            tm,
        )

    def group_at(turn):
        away = jnp.where(turn < 2, turn, 5 - turn)
        return wrap(z // 4 + away, GROUPS)

    def lift_time(group, rim, r):
        at = 4 * r
        p0, p1, p2, p3 = [
            held[pl.ds(group * 512 + r * 4 + q, 8, stride=64), :] for q in range(4)
        ]
        d1 = detail(p0, p1, p2)
        ahead = jnp.where(
            lane == 127,
            pltpu.roll(rim, 125 - at, 1) * has_next_band,
            pltpu.roll(p0, 127, 1),
        )
        d3 = detail(p2, p3, ahead)
        rim_detail = pltpu.roll(rim, 128 - at, 1) if at else rim
        d3_prev = (rim_detail - 0.5 * p0) * has_prev_band
        s0 = smooth(p0, jnp.where(lane == 0, d3_prev, pltpu.roll(d3, 1, 1)), d1)
        s2 = smooth(p2, d1, d3)
        next_s0 = (pltpu.roll(rim, 124 - at, 1) + 0.25 * d3) * has_next_band
        second = detail(s0, s2, jnp.where(lane == 127, next_s0, pltpu.roll(s0, 127, 1)))
        rim_second = pltpu.roll(rim, 127 - at, 1)
        second_prev = (rim_second + 0.25 * d3_prev - 0.5 * s0) * has_prev_band
        first = smooth(
            s0, jnp.where(lane == 0, second_prev, pltpu.roll(second, 1, 1)), second
        )
        values = (s0, d1, s2, d3, first, second)
        for slot, value in enumerate(values):
            lifted[slot, r, span(group)] = value
        return values

    @pl.loop(0, GROUPS)
    def _(turn):
        group = group_at(turn)
        settle(held.at[pl.ds(0, ROWS // GROUPS)], arrive_sems.at[group])
        rim = rims[span(group)]
        ends = {r: lift_time(group, rim, r) for r in (0, 1, 2, 10, 11, 12, 13, 14, 15)}
        for slot, value in enumerate(ends[0]):
            ahead_send[slot, span(group)] = value
        for slot, plane in enumerate((4, 5)):
            value = {r: values[plane] for r, values in ends.items()}
            ahead_send[6 + slot, span(group)] = value[0] + 0.25 * detail(value[0], value[1], value[2])
            d5 = detail(value[10], value[11], value[12])
            d6 = detail(value[12], value[13], value[14])
            s6 = smooth(value[12], d5, d6)
            back_send[4 + slot, span(group)] = value[14] + 0.25 * d6 - 0.5 * s6
        for slot, plane in enumerate((1, 3, 4, 5)):
            back_send[slot, span(group)] = ends[15][plane] - 0.5 * ends[14][plane]
        line_copy(0, group).start()
        line_copy(1, group).start()

    @pl.loop(0, GROUPS)
    def _(turn):
        group = group_at(turn)
        rim = rims[span(group)]
        for r in range(3, 10):
            lift_time(group, rim, r)

    def put(group, r, q, value, gains):
        wave[pl.ds(group * 512 + r * 4 + q, 8, stride=64), :] = value
        square = value * value
        capped = [jnp.minimum(square, 4.0 ** (4 - p)) for p in range(PLANES + 1)]
        for p in range(PLANES):
            gains[p] = gains[p] + (capped[p] - capped[p + 1])

    @pl.loop(0, GROUPS)
    def _(turn):
        group = group_at(turn)
        gains = [jnp.zeros((8, 128), jnp.float32) for _ in range(PLANES)]
        for slot in range(6):
            values = [lifted[slot, r, span(group)] for r in range(15)]
            details = [
                detail(values[2 * i], values[2 * i + 1], values[2 * i + 2]) for i in range(7)
            ]
            if slot < 4:
                for i in range(7):
                    put(group, 2 * i + 1, slot, details[i], gains)
            if slot in (0, 2):
                continue
            smooths = [None] + [
                smooth(values[2 * i], details[i - 1], details[i]) for i in range(1, 7)
            ]
            if slot < 4:
                for i in range(1, 7):
                    put(group, 2 * i, slot, smooths[i], gains)
                continue
            second_one = detail(smooths[2], smooths[3], smooths[4])
            second_two = detail(smooths[4], smooths[5], smooths[6])
            q = (slot - 4) * 2
            put(group, 6, q, second_one, gains)
            put(group, 8, q, smooth(smooths[4], second_one, second_two), gains)
            put(group, 10, q, second_two, gains)
            kept_edges = (smooths[1], smooths[2], second_one, smooths[6], second_two)
            for n, value in enumerate(kept_edges):
                edges[slot - 4, n, span(group)] = value
        for p in range(PLANES):
            gain_acc[p, span(group)] = gains[p]

    @pl.loop(0, GROUPS)
    def _(turn):
        group = group_at(turn)
        line_copy(0, group).wait_recv()
        line_copy(1, group).wait_recv()
        gains = [gain_acc[p, span(group)] for p in range(PLANES)]
        for slot in range(6):
            first, early, third, before, odd, even, last = [
                lifted[slot, r, span(group)] for r in (0, 1, 2, 12, 13, 14, 15)
            ]
            ahead = ahead_recv[slot, span(group)] * has_next_line
            detail_last = detail(even, last, ahead)
            if slot < 4:
                put(group, 15, slot, detail_last, gains)
            if slot in (0, 2):
                continue
            back_slot = {1: 0, 3: 1, 4: 2, 5: 3}[slot]
            behind = (back_recv[back_slot, span(group)] - 0.5 * first) * has_prev_line
            smooth_first = smooth(first, behind, detail(first, early, third))
            smooth_last = smooth(even, detail(before, odd, even), detail_last)
            if slot < 4:
                put(group, 0, slot, smooth_first, gains)
                put(group, 14, slot, smooth_last, gains)
                continue
            k = slot - 4
            q = k * 2
            s1, s2, second_one, s6, second_two = [edges[k, n, span(group)] for n in range(5)]
            s8 = (ahead_recv[6 + k, span(group)] + 0.25 * detail_last) * has_next_line
            second_last = detail(s6, smooth_last, s8)
            second_first = detail(smooth_first, s1, s2)
            behind_two = (
                back_recv[4 + k, span(group)] + 0.25 * behind - 0.5 * smooth_first
            ) * has_prev_line
            put(group, 0, q, smooth(smooth_first, behind_two, second_first), gains)
            put(group, 2, q, second_first, gains)
            put(group, 4, q, smooth(s2, second_first, second_one), gains)
            put(group, 12, q, smooth(s6, second_two, second_last), gains)
            put(group, 14, q, second_last, gains)

        sums = [
            jnp.broadcast_to(jnp.sum(gains[p], axis=1, keepdims=True), (8, 128))
            for p in range(PLANES)
        ]
        rates = [rate_cols[p, span(group)] for p in range(PLANES)]

        @pl.loop(0, SLOPE_ROWS, unroll=4)
        def _(row):
            total = kept_acc[row]
            for p in range(PLANES):
                total = total + jnp.where(sums[p] >= bars[row, p, span(group)], rates[p], 0.0)
            kept_acc[row] = total

    out = pltpu.make_async_copy(wave.at[pl.ds(0, ROWS)], w_ref, own_sems.at[0])
    out.start()

    half = SLOPE_ROWS // 2
    kept_rows[:, 0:128] = jnp.sum(kept_acc[0:half], axis=1).astype(jnp.int32)
    kept_rows[:, 128:256] = jnp.sum(kept_acc[half:SLOPE_ROWS], axis=1).astype(jnp.int32)
    place = peer_place[0] + tm

    for step in PLANE_STEPS:
        to_line, to_tm, to_place = plane_peer(step)
        remote(
            row_of(kept_rows, to_place),
            row_of(plane_slots, place),
            tree_sems.at[0, 0],
            tree_sems.at[1, 0],
            to_line,
            to_tm,
        ).start()
    plane_slots[pl.ds(place, 1)] = kept_rows[pl.ds(place, 1)]
    settle(held.at[pl.ds(0, 30)], tree_sems.at[1, 0])
    ring_row[...] = jnp.sum(plane_slots[...], axis=0, keepdims=True)

    for step in RING_STEPS + [0]:
        plane = wrap(z + step, 16) * 8 + spot
        for to in (plane, plane + 1 - 2 * core):
            if step == 0 and to is plane:
                continue
            remote(
                ring_row,
                row_of(ring_slots, z * 2 + core),
                tree_sems.at[0, 1],
                tree_sems.at[1, 1],
                to,
                tm,
            ).start()
    ring_slots[pl.ds(z * 2 + core, 1)] = ring_row[...]
    settle(held.at[pl.ds(0, 62)], tree_sems.at[1, 1])
    kept = jnp.sum(ring_slots[...], axis=0, keepdims=True)
    limit = target_ref[0] * (SHOTS * LINES * BANDS)
    lane256 = lax.broadcasted_iota(jnp.int32, (1, 256), 1)
    grid_row = place * 128 + jnp.where(lane256 < 128, lane256, lane256 + 2**BISECT // 2 - 128)
    above = jnp.where((kept > limit) & (grid_row > 0), 1.0, 0.0)
    count_row[...] = jnp.broadcast_to(jnp.sum(above, axis=1, keepdims=True), (1, 128))

    for step in PLANE_STEPS:
        to_line, to_tm, _ = plane_peer(step)
        remote(
            count_row,
            row_of(count_slots, place),
            tree_sems.at[0, 2],
            tree_sems.at[1, 2],
            to_line,
            to_tm,
        ).start()
    count_slots[pl.ds(place, 1)] = count_row[...]
    settle(count_slots.at[pl.ds(0, 15)], tree_sems.at[1, 2])
    chosen = 1.0 + jnp.sum(count_slots[...], axis=0, keepdims=True)
    slope_now = jnp.exp2(slope_floor + chosen * (slope_span / 2**BISECT))
    shrink_ref[...] = jnp.sqrt(slope_now * rate_cols[PLANES] / rate_scale)

    out.wait()
    settle(held.at[pl.ds(0, ROWS - 16)], send_sem.at[0])
    band_up.wait_send()
    band_down.wait_send()
    settle(rim_plane.at[pl.ds(0, 7)], rim_sems.at[0, 2])
    settle(rim_ring.at[pl.ds(0, 15)], rim_sems.at[0, 3])

    @pl.loop(0, GROUPS)
    def _(group):
        for way in range(2):
            line_copy(way, group).wait_send()

    settle(held.at[pl.ds(0, 30)], tree_sems.at[0, 0])
    settle(held.at[pl.ds(0, 62)], tree_sems.at[0, 1])
    settle(count_slots.at[pl.ds(0, 15)], tree_sems.at[0, 2])


def transform(rows, rates, byte_target):
    vmem = pl.BlockSpec(memory_space=pltpu.VMEM)
    hbm = pl.BlockSpec(memory_space=pl.ANY)
    rows, rates = [pltpu.with_memory_space_constraint(a, pltpu.HBM) for a in (rows, rates)]
    f32 = jnp.float32
    return pl.pallas_call(
        kernel,
        out_shape=[
            jax.ShapeDtypeStruct((ROWS, 128), f32),
            jax.ShapeDtypeStruct((SHOTS, 128), f32),
        ],
        in_specs=[hbm, hbm, pl.BlockSpec(memory_space=pltpu.SMEM)],
        out_specs=[hbm, vmem],
        scratch_shapes=[
            pltpu.VMEM((ROWS + 64, 128), f32),
            pltpu.VMEM((ROWS + 64, 128), f32),
            pltpu.VMEM((6, 16, SHOTS, 128), f32),
            pltpu.VMEM((ROWS + 64, 128), f32),
            pltpu.VMEM((16, 128), f32),
            pltpu.VMEM((2, 16, 128), f32),
            pltpu.VMEM((16, 128), f32),
            pltpu.VMEM((8, 16, 128), f32),
            pltpu.VMEM((16, 128), f32),
            pltpu.VMEM((SHOTS + 8, 128), f32),
            pltpu.VMEM((8, SHOTS, 128), f32),
            pltpu.VMEM((8, SHOTS, 128), f32),
            pltpu.VMEM((6, SHOTS, 128), f32),
            pltpu.VMEM((6, SHOTS, 128), f32),
            pltpu.VMEM((PLANES, SHOTS), jnp.int32),
            pltpu.VMEM((SLOPE_ROWS, PLANES, SHOTS, 128), f32),
            pltpu.VMEM((2, 5, SHOTS, 128), f32),
            pltpu.VMEM((PLANES, SHOTS, 128), f32),
            pltpu.VMEM((PLANES + 1, SHOTS, 128), f32),
            pltpu.VMEM((SLOPE_ROWS, 8, 128), f32),
            pltpu.VMEM((16, 256), jnp.int32),
            pltpu.VMEM((16, 256), jnp.int32),
            pltpu.VMEM((1, 256), jnp.int32),
            pltpu.VMEM((32, 256), jnp.int32),
            pltpu.VMEM((1, 128), f32),
            pltpu.VMEM((16, 128), f32),
            pltpu.SemaphoreType.DMA((2,)),
            pltpu.SemaphoreType.DMA((1,)),
            pltpu.SemaphoreType.DMA((GROUPS,)),
            pltpu.SemaphoreType.DMA((2, 4)),
            pltpu.SemaphoreType.DMA((2, 2, GROUPS)),
            pltpu.SemaphoreType.DMA((2, 3)),
        ],
        compiler_params=pltpu.CompilerParams(
            collective_id=1, has_side_effects=True, vmem_limit_bytes=24 * 2**20
        ),
        name="transform",
    )(rows, rates, byte_target)


def threshold_kernel(wave_ref, shrink_ref, o_ref, out, sems):
    copies = []
    for chunk in range(CHUNKS):
        for shot in range(chunk * SHOTS // CHUNKS, (chunk + 1) * SHOTS // CHUNKS):
            wavelet = wave_ref[shot * 64 : shot * 64 + 64, :]
            limit = jnp.broadcast_to(shrink_ref[shot : shot + 1, :], (64, 128))
            clipped = jnp.minimum(jnp.maximum(wavelet, -limit), limit)
            out[shot * 64 : shot * 64 + 64, :] = wavelet - clipped
        rows = pl.ds(chunk * ROWS // CHUNKS, ROWS // CHUNKS)
        copy = pltpu.make_async_copy(out.at[rows], o_ref.at[rows], sems.at[chunk])
        copy.start()
        copies.append(copy)
    for copy in copies:
        copy.wait()


def threshold(wave, shrink):
    vmem = pl.BlockSpec(memory_space=pltpu.VMEM)
    return pl.pallas_call(
        threshold_kernel,
        out_shape=jax.ShapeDtypeStruct((ROWS, 128), jnp.float32),
        in_specs=[vmem, vmem],
        out_specs=pl.BlockSpec(memory_space=pl.ANY),
        scratch_shapes=[
            pltpu.VMEM((ROWS, 128), jnp.float32),
            pltpu.SemaphoreType.DMA((CHUNKS,)),
        ],
        compiler_params=pltpu.CompilerParams(vmem_limit_bytes=24 * 2**20),
        name="threshold",
    )(wave, shrink)


def body(traces, rates, byte_target):
    width = traces.shape[3]
    rows = traces.reshape(ROWS, width)
    wave, shrink = transform(rows, rates.reshape(PLANES, SHOTS), byte_target)
    return threshold(wave, shrink).reshape(SHOTS, 16, 4, width)


def solution(mesh):
    return jax.shard_map(
        body,
        mesh=mesh,
        in_specs=(P("line", None, None, "tm"), P("line", "tm", None, None), P()),
        out_specs=P(None, "line", None, "tm"),
        check_vma=False,
    )
```

```python
import jax
import jax.numpy as jnp
from jax import lax
from jax.experimental import pallas as pl
from jax.experimental.pallas import tpu as pltpu
from jax.sharding import PartitionSpec as P

PLANES = 8
BISECT = 12
LINES = 128
BANDS = 4
SHOTS = 32
GROUPS = 4
ROWS = 2048
CHUNKS = 8
FIRST = 32
SECOND = 112
SLOPE_ROWS = 2**BISECT // 128
MESH = pl.DeviceIdType.MESH

slope_floor = -12.0
slope_span = 32.0
rate_scale = 65536.0

PLANE_STEPS = sorted(
    [(dx, dy) for dx in range(4) for dy in range(4)][1:],
    key=lambda s: (-(min(s[0], 4 - s[0]) + min(s[1], 4 - s[1])), s),
)
RING_STEPS = sorted(range(1, 16), key=lambda s: -min(s, 16 - s))


def remote(src, dst, ssem, rsem, line, tm):
    return pltpu.make_async_remote_copy(
        src_ref=src,
        dst_ref=dst,
        send_sem=ssem,
        recv_sem=rsem,
        device_id=(line, tm),
        device_id_type=MESH,
    )


def settle(ref, sem):
    pltpu.make_async_copy(ref, ref, sem).wait()


def wrap(value, count):
    return jnp.where(value >= count, value - count, value)


def detail(even_part, odd_part, ahead_even):
    return odd_part - 0.5 * (even_part + ahead_even)


def smooth(even_part, behind, details):
    return even_part + 0.25 * (behind + details)


def kernel(
    x_ref,
    rates_ref,
    target_ref,
    w_ref,
    shrink_ref,
    local,
    held,
    lifted,
    wave,
    rim_own,
    rim_bands,
    rim_merged,
    rim_plane,
    rim_ring,
    rims,
    ahead_send,
    ahead_recv,
    back_send,
    back_recv,
    rate_table,
    bars,
    edges,
    gain_acc,
    rate_cols,
    kept_acc,
    kept_rows,
    plane_slots,
    ring_row,
    ring_slots,
    count_row,
    count_slots,
    own_sems,
    send_sem,
    arrive_sems,
    rim_sems,
    line_sems,
    tree_sems,
):
    line = lax.axis_index("line")
    tm = lax.axis_index("tm")
    z = line // 8
    x = (line // 2) % 4
    core = line % 2
    spot = line % 8

    peer_place = [wrap(x + k, 4) * 4 for k in range(4)]
    peer_x = [(z * 4 + wrap(x + k, 4)) * 2 for k in range(4)]
    peer_tm = [wrap(tm + k, 4) for k in range(4)]

    def plane_peer(step):
        dx, dy = step
        return peer_x[dx] + core, peer_tm[dy], peer_place[dx] + peer_tm[dy]

    def span(group):
        return pl.ds(pl.multiple_of(group * 8, 8), 8)

    def row_of(ref, index):
        return ref.at[pl.ds(index, 1)]

    fetch = pltpu.make_async_copy(x_ref, local.at[pl.ds(0, ROWS)], own_sems.at[0])
    fetch.start()
    fetch_rates = pltpu.make_async_copy(rates_ref, rate_table, own_sems.at[1])
    fetch_rates.start()

    up, down = peer_tm[1], peer_tm[3]
    bar = pltpu.get_barrier_semaphore()

    @pl.loop(0, 15)
    def _(i):
        near = 8 - (i + 1) // 2
        step = jnp.where(i % 2 == 0, near, 16 - near)
        plane = wrap(z + step, 16) * 8
        for k in range(8):
            pl.semaphore_signal(bar, inc=1, device_id=(plane + k, tm), device_id_type=MESH)

    for k in range(1, 8):
        pl.semaphore_signal(
            bar, inc=1, device_id=(z * 8 + wrap(spot + k, 8), tm), device_id_type=MESH
        )
    for to in (up, down):
        pl.semaphore_signal(bar, inc=1, device_id=(line, to), device_id_type=MESH)

    pl.semaphore_wait(bar, LINES + 1)

    mine = held.at[pl.ds(pl.multiple_of(line * 16, 16), 16)]
    pltpu.make_async_copy(
        x_ref.at[pl.ds(pl.multiple_of(line * 16, 16), 16)], mine, arrive_sems.at[z // 4]
    ).start()

    def scatter(first, last):
        @pl.loop(first, last)
        def _(i):
            near = (i + 1) // 2
            to = wrap(line + jnp.where(i % 2 == 0, 64 - near, 64 + near), LINES)
            remote(
                x_ref.at[pl.ds(pl.multiple_of(to * 16, 16), 16)],
                mine,
                send_sem.at[0],
                arrive_sems.at[z // 4],
                to,
                tm,
            ).start()

    scatter(0, FIRST)

    lane = lax.broadcasted_iota(jnp.int32, (8, 128), 1)
    sub = lax.broadcasted_iota(jnp.int32, (8, 128), 0)
    fetch.wait()

    @pl.loop(0, 16)
    def _(plane):
        total = jnp.zeros((8, 128), jnp.float32)
        for block in range(4):
            p0, p1, p2, p3 = [
                local[pl.ds(plane * 128 + block * 32 + q, 8, stride=4), :] for q in range(4)
            ]
            d1 = detail(p0, p1, p2)
            d3 = detail(p2, p3, pltpu.roll(p0, 127, 1))
            s0 = smooth(p0, pltpu.roll(d3, 1, 1), d1)
            rim_detail = p3 - 0.5 * p2
            rim_second = p2 + 0.25 * d1 - 0.5 * s0
            rim_smooth = p0 + 0.25 * d1
            columns = (
                rim_detail[:, 127:128],
                rim_second[:, 127:128],
                p0[:, 0:1],
                rim_smooth[:, 0:1],
            )
            for v, column in enumerate(columns):
                at = (sub + block * 8) * 4 + v
                total = jnp.where(lane == at, jnp.broadcast_to(column, (8, 128)), total)
        rim_own[pl.ds(plane, 1), :] = jnp.sum(total, axis=0, keepdims=True)

    band_up = remote(rim_own, rim_bands.at[0], rim_sems.at[0, 0], rim_sems.at[1, 0], line, up)
    band_down = remote(rim_own, rim_bands.at[1], rim_sems.at[0, 1], rim_sems.at[1, 1], line, down)
    band_up.start()
    band_down.start()

    band_up.wait_recv()
    band_down.wait_recv()
    lane16 = lax.broadcasted_iota(jnp.int32, (16, 128), 1)
    rim_merged[...] = jnp.where(lane16 % 4 < 2, rim_bands[0], rim_bands[1])
    for step in RING_STEPS:
        to = wrap(z + step, 16)
        remote(
            row_of(rim_merged, to),
            row_of(rim_ring, z),
            rim_sems.at[0, 3],
            rim_sems.at[1, 3],
            to * 8 + spot,
            tm,
        ).start()
    rim_ring[pl.ds(z, 1), :] = rim_merged[pl.ds(z, 1), :]

    scatter(FIRST, SECOND)

    settle(rim_ring.at[pl.ds(0, 15)], rim_sems.at[1, 3])
    for k in range(1, 8):
        remote(
            rim_ring,
            rim_plane.at[spot],
            rim_sems.at[0, 2],
            rim_sems.at[1, 2],
            z * 8 + wrap(spot + k, 8),
            tm,
        ).start()
    rim_plane[spot] = rim_ring[...]

    scatter(SECOND, LINES - 1)

    fetch_rates.wait()
    for group in range(GROUPS):
        total = jnp.zeros((8, 128), jnp.float32)
        for plane in range(PLANES):
            rate_row = rate_table[plane : plane + 1, :].astype(jnp.float32)
            picked = jnp.where(
                lane[:, :SHOTS] == sub[:, :SHOTS] + group * 8,
                jnp.broadcast_to(rate_row, (8, SHOTS)),
                0.0,
            )
            column = jnp.broadcast_to(jnp.sum(picked, axis=1, keepdims=True), (8, 128))
            rate_cols[plane, group * 8 : group * 8 + 8] = column
            total = total + column
        rate_cols[PLANES, group * 8 : group * 8 + 8] = total

    @pl.loop(0, SLOPE_ROWS)
    def _(row):
        kept_acc[row] = jnp.zeros((8, 128), jnp.float32)
        grid_index = (lane + row * 128).astype(jnp.float32)
        slope = jnp.exp2(slope_floor + grid_index * (slope_span / 2**BISECT))
        for plane in range(PLANES):
            for group in range(GROUPS):
                column = rate_cols[plane, group * 8 : group * 8 + 8]
                bars[row, plane, group * 8 : group * 8 + 8] = slope * column

    settle(rim_plane.at[pl.ds(0, 7)], rim_sems.at[1, 2])
    packed = jnp.zeros((16, 128), jnp.float32)
    for k in range(8):
        turned = pltpu.roll(rim_plane[k], lax.rem((k + 8 - spot) * 16, 128), 1)
        packed = jnp.where(lane16 // 16 == k, turned, packed)

    rims[pl.ds(0, 16, stride=2), :] = packed
    rims[pl.ds(1, 16, stride=2), :] = pltpu.roll(packed, 64, 1)

    has_prev_band = jnp.where(tm > 0, 1.0, 0.0)
    has_next_band = jnp.where(tm < BANDS - 1, 1.0, 0.0)
    has_prev_line = jnp.where(line > 0, 1.0, 0.0)
    has_next_line = jnp.where(line < LINES - 1, 1.0, 0.0)
    line_up = wrap(line + 1, LINES)
    line_down = wrap(line + LINES - 1, LINES)

    def line_copy(way, group):
        if way == 0:
            return remote(
                ahead_send.at[:, span(group)],
                ahead_recv.at[:, span(group)],
                line_sems.at[0, 0, group],
                line_sems.at[1, 0, group],
                line_down,
                tm,
            )
        return remote(
            back_send.at[:, span(group)],
            back_recv.at[:, span(group)],
            line_sems.at[0, 1, group],
            line_sems.at[1, 1, group],
            line_up,
            tm,
        )

    def group_at(turn):
        away = jnp.where(turn < 2, turn, 5 - turn)
        return wrap(z // 4 + away, GROUPS)

    def lift_time(group, rim, r):
        at = 4 * r
        p0, p1, p2, p3 = [
            held[pl.ds(group * 512 + r * 4 + q, 8, stride=64), :] for q in range(4)
        ]
        d1 = detail(p0, p1, p2)
        ahead = jnp.where(
            lane == 127,
            pltpu.roll(rim, 125 - at, 1) * has_next_band,
            pltpu.roll(p0, 127, 1),
        )
        d3 = detail(p2, p3, ahead)
        rim_detail = pltpu.roll(rim, 128 - at, 1) if at else rim
        d3_prev = (rim_detail - 0.5 * p0) * has_prev_band
        s0 = smooth(p0, jnp.where(lane == 0, d3_prev, pltpu.roll(d3, 1, 1)), d1)
        s2 = smooth(p2, d1, d3)
        next_s0 = (pltpu.roll(rim, 124 - at, 1) + 0.25 * d3) * has_next_band
        second = detail(s0, s2, jnp.where(lane == 127, next_s0, pltpu.roll(s0, 127, 1)))
        rim_second = pltpu.roll(rim, 127 - at, 1)
        second_prev = (rim_second + 0.25 * d3_prev - 0.5 * s0) * has_prev_band
        first = smooth(
            s0, jnp.where(lane == 0, second_prev, pltpu.roll(second, 1, 1)), second
        )
        values = (s0, d1, s2, d3, first, second)
        for slot, value in enumerate(values):
            lifted[slot, r, span(group)] = value
        return values

    @pl.loop(0, GROUPS)
    def _(turn):
        group = group_at(turn)
        settle(held.at[pl.ds(0, ROWS // GROUPS)], arrive_sems.at[group])
        rim = rims[span(group)]
        ends = {r: lift_time(group, rim, r) for r in (0, 1, 2, 10, 11, 12, 13, 14, 15)}
        for slot, value in enumerate(ends[0]):
            ahead_send[slot, span(group)] = value
        for slot, plane in enumerate((4, 5)):
            value = {r: values[plane] for r, values in ends.items()}
            ahead_send[6 + slot, span(group)] = value[0] + 0.25 * detail(value[0], value[1], value[2])
            d5 = detail(value[10], value[11], value[12])
            d6 = detail(value[12], value[13], value[14])
            s6 = smooth(value[12], d5, d6)
            back_send[4 + slot, span(group)] = value[14] + 0.25 * d6 - 0.5 * s6
        for slot, plane in enumerate((1, 3, 4, 5)):
            back_send[slot, span(group)] = ends[15][plane] - 0.5 * ends[14][plane]
        line_copy(0, group).start()
        line_copy(1, group).start()

    @pl.loop(0, GROUPS)
    def _(turn):
        group = group_at(turn)
        rim = rims[span(group)]
        for r in range(3, 10):
            lift_time(group, rim, r)

    def put(group, r, q, value, gains):
        wave[pl.ds(group * 512 + r * 4 + q, 8, stride=64), :] = value
        square = value * value
        capped = [jnp.minimum(square, 4.0 ** (4 - p)) for p in range(PLANES + 1)]
        for p in range(PLANES):
            gains[p] = gains[p] + (capped[p] - capped[p + 1])

    @pl.loop(0, GROUPS)
    def _(turn):
        group = group_at(turn)
        gains = [jnp.zeros((8, 128), jnp.float32) for _ in range(PLANES)]
        for slot in range(6):
            values = [lifted[slot, r, span(group)] for r in range(15)]
            details = [
                detail(values[2 * i], values[2 * i + 1], values[2 * i + 2]) for i in range(7)
            ]
            if slot < 4:
                for i in range(7):
                    put(group, 2 * i + 1, slot, details[i], gains)
            if slot in (0, 2):
                continue
            smooths = [None] + [
                smooth(values[2 * i], details[i - 1], details[i]) for i in range(1, 7)
            ]
            if slot < 4:
                for i in range(1, 7):
                    put(group, 2 * i, slot, smooths[i], gains)
                continue
            second_one = detail(smooths[2], smooths[3], smooths[4])
            second_two = detail(smooths[4], smooths[5], smooths[6])
            q = (slot - 4) * 2
            put(group, 6, q, second_one, gains)
            put(group, 8, q, smooth(smooths[4], second_one, second_two), gains)
            put(group, 10, q, second_two, gains)
            kept_edges = (smooths[1], smooths[2], second_one, smooths[6], second_two)
            for n, value in enumerate(kept_edges):
                edges[slot - 4, n, span(group)] = value
        for p in range(PLANES):
            gain_acc[p, span(group)] = gains[p]

    @pl.loop(0, GROUPS)
    def _(turn):
        group = group_at(turn)
        line_copy(0, group).wait_recv()
        line_copy(1, group).wait_recv()
        gains = [gain_acc[p, span(group)] for p in range(PLANES)]
        for slot in range(6):
            first, early, third, before, odd, even, last = [
                lifted[slot, r, span(group)] for r in (0, 1, 2, 12, 13, 14, 15)
            ]
            ahead = ahead_recv[slot, span(group)] * has_next_line
            detail_last = detail(even, last, ahead)
            if slot < 4:
                put(group, 15, slot, detail_last, gains)
            if slot in (0, 2):
                continue
            back_slot = {1: 0, 3: 1, 4: 2, 5: 3}[slot]
            behind = (back_recv[back_slot, span(group)] - 0.5 * first) * has_prev_line
            smooth_first = smooth(first, behind, detail(first, early, third))
            smooth_last = smooth(even, detail(before, odd, even), detail_last)
            if slot < 4:
                put(group, 0, slot, smooth_first, gains)
                put(group, 14, slot, smooth_last, gains)
                continue
            k = slot - 4
            q = k * 2
            s1, s2, second_one, s6, second_two = [edges[k, n, span(group)] for n in range(5)]
            s8 = (ahead_recv[6 + k, span(group)] + 0.25 * detail_last) * has_next_line
            second_last = detail(s6, smooth_last, s8)
            second_first = detail(smooth_first, s1, s2)
            behind_two = (
                back_recv[4 + k, span(group)] + 0.25 * behind - 0.5 * smooth_first
            ) * has_prev_line
            put(group, 0, q, smooth(smooth_first, behind_two, second_first), gains)
            put(group, 2, q, second_first, gains)
            put(group, 4, q, smooth(s2, second_first, second_one), gains)
            put(group, 12, q, smooth(s6, second_two, second_last), gains)
            put(group, 14, q, second_last, gains)

        sums = [
            jnp.broadcast_to(jnp.sum(gains[p], axis=1, keepdims=True), (8, 128))
            for p in range(PLANES)
        ]
        rates = [rate_cols[p, span(group)] for p in range(PLANES)]

        @pl.loop(0, SLOPE_ROWS, unroll=4)
        def _(row):
            total = kept_acc[row]
            for p in range(PLANES):
                total = total + jnp.where(sums[p] >= bars[row, p, span(group)], rates[p], 0.0)
            kept_acc[row] = total

    out = pltpu.make_async_copy(wave.at[pl.ds(0, ROWS)], w_ref, own_sems.at[0])
    out.start()

    half = SLOPE_ROWS // 2
    kept_rows[:, 0:128] = jnp.sum(kept_acc[0:half], axis=1).astype(jnp.int32)
    kept_rows[:, 128:256] = jnp.sum(kept_acc[half:SLOPE_ROWS], axis=1).astype(jnp.int32)
    place = peer_place[0] + tm

    for step in PLANE_STEPS:
        to_line, to_tm, to_place = plane_peer(step)
        remote(
            row_of(kept_rows, to_place),
            row_of(plane_slots, place),
            tree_sems.at[0, 0],
            tree_sems.at[1, 0],
            to_line,
            to_tm,
        ).start()
    plane_slots[pl.ds(place, 1)] = kept_rows[pl.ds(place, 1)]
    settle(held.at[pl.ds(0, 30)], tree_sems.at[1, 0])
    ring_row[...] = jnp.sum(plane_slots[...], axis=0, keepdims=True)

    for step in RING_STEPS + [0]:
        plane = wrap(z + step, 16) * 8 + spot
        for to in (plane, plane + 1 - 2 * core):
            if step == 0 and to is plane:
                continue
            remote(
                ring_row,
                row_of(ring_slots, z * 2 + core),
                tree_sems.at[0, 1],
                tree_sems.at[1, 1],
                to,
                tm,
            ).start()
    ring_slots[pl.ds(z * 2 + core, 1)] = ring_row[...]
    settle(held.at[pl.ds(0, 62)], tree_sems.at[1, 1])
    kept = jnp.sum(ring_slots[...], axis=0, keepdims=True)
    limit = target_ref[0] * (SHOTS * LINES * BANDS)
    lane256 = lax.broadcasted_iota(jnp.int32, (1, 256), 1)
    grid_row = place * 128 + jnp.where(lane256 < 128, lane256, lane256 + 2**BISECT // 2 - 128)
    above = jnp.where((kept > limit) & (grid_row > 0), 1.0, 0.0)
    count_row[...] = jnp.broadcast_to(jnp.sum(above, axis=1, keepdims=True), (1, 128))

    for step in PLANE_STEPS:
        to_line, to_tm, _ = plane_peer(step)
        remote(
            count_row,
            row_of(count_slots, place),
            tree_sems.at[0, 2],
            tree_sems.at[1, 2],
            to_line,
            to_tm,
        ).start()
    count_slots[pl.ds(place, 1)] = count_row[...]
    settle(count_slots.at[pl.ds(0, 15)], tree_sems.at[1, 2])
    chosen = 1.0 + jnp.sum(count_slots[...], axis=0, keepdims=True)
    slope_now = jnp.exp2(slope_floor + chosen * (slope_span / 2**BISECT))
    shrink_ref[...] = jnp.sqrt(slope_now * rate_cols[PLANES] / rate_scale)

    out.wait()
    settle(held.at[pl.ds(0, ROWS - 16)], send_sem.at[0])
    band_up.wait_send()
    band_down.wait_send()
    settle(rim_plane.at[pl.ds(0, 7)], rim_sems.at[0, 2])
    settle(rim_ring.at[pl.ds(0, 15)], rim_sems.at[0, 3])

    @pl.loop(0, GROUPS)
    def _(group):
        for way in range(2):
            line_copy(way, group).wait_send()

    settle(held.at[pl.ds(0, 30)], tree_sems.at[0, 0])
    settle(held.at[pl.ds(0, 62)], tree_sems.at[0, 1])
    settle(count_slots.at[pl.ds(0, 15)], tree_sems.at[0, 2])


def transform(rows, rates, byte_target):
    vmem = pl.BlockSpec(memory_space=pltpu.VMEM)
    hbm = pl.BlockSpec(memory_space=pl.ANY)
    rows, rates = [pltpu.with_memory_space_constraint(a, pltpu.HBM) for a in (rows, rates)]
    f32 = jnp.float32
    return pl.pallas_call(
        kernel,
        out_shape=[
            jax.ShapeDtypeStruct((ROWS, 128), f32),
            jax.ShapeDtypeStruct((SHOTS, 128), f32),
        ],
        in_specs=[hbm, hbm, pl.BlockSpec(memory_space=pltpu.SMEM)],
        out_specs=[hbm, vmem],
        scratch_shapes=[
            pltpu.VMEM((ROWS + 64, 128), f32),
            pltpu.VMEM((ROWS + 64, 128), f32),
            pltpu.VMEM((6, 16, SHOTS, 128), f32),
            pltpu.VMEM((ROWS + 64, 128), f32),
            pltpu.VMEM((16, 128), f32),
            pltpu.VMEM((2, 16, 128), f32),
            pltpu.VMEM((16, 128), f32),
            pltpu.VMEM((8, 16, 128), f32),
            pltpu.VMEM((16, 128), f32),
            pltpu.VMEM((SHOTS + 8, 128), f32),
            pltpu.VMEM((8, SHOTS, 128), f32),
            pltpu.VMEM((8, SHOTS, 128), f32),
            pltpu.VMEM((6, SHOTS, 128), f32),
            pltpu.VMEM((6, SHOTS, 128), f32),
            pltpu.VMEM((PLANES, SHOTS), jnp.int32),
            pltpu.VMEM((SLOPE_ROWS, PLANES, SHOTS, 128), f32),
            pltpu.VMEM((2, 5, SHOTS, 128), f32),
            pltpu.VMEM((PLANES, SHOTS, 128), f32),
            pltpu.VMEM((PLANES + 1, SHOTS, 128), f32),
            pltpu.VMEM((SLOPE_ROWS, 8, 128), f32),
            pltpu.VMEM((16, 256), jnp.int32),
            pltpu.VMEM((16, 256), jnp.int32),
            pltpu.VMEM((1, 256), jnp.int32),
            pltpu.VMEM((32, 256), jnp.int32),
            pltpu.VMEM((1, 128), f32),
            pltpu.VMEM((16, 128), f32),
            pltpu.SemaphoreType.DMA((2,)),
            pltpu.SemaphoreType.DMA((1,)),
            pltpu.SemaphoreType.DMA((GROUPS,)),
            pltpu.SemaphoreType.DMA((2, 4)),
            pltpu.SemaphoreType.DMA((2, 2, GROUPS)),
            pltpu.SemaphoreType.DMA((2, 3)),
        ],
        compiler_params=pltpu.CompilerParams(
            collective_id=1, has_side_effects=True, vmem_limit_bytes=24 * 2**20
        ),
        name="transform",
    )(rows, rates, byte_target)


def threshold_kernel(wave_ref, shrink_ref, o_ref, out, sems):
    copies = []
    for chunk in range(CHUNKS):
        for shot in range(chunk * SHOTS // CHUNKS, (chunk + 1) * SHOTS // CHUNKS):
            wavelet = wave_ref[shot * 64 : shot * 64 + 64, :]
            limit = jnp.broadcast_to(shrink_ref[shot : shot + 1, :], (64, 128))
            clipped = jnp.minimum(jnp.maximum(wavelet, -limit), limit)
            out[shot * 64 : shot * 64 + 64, :] = wavelet - clipped
        rows = pl.ds(chunk * ROWS // CHUNKS, ROWS // CHUNKS)
        copy = pltpu.make_async_copy(out.at[rows], o_ref.at[rows], sems.at[chunk])
        copy.start()
        copies.append(copy)
    for copy in copies:
        copy.wait()


def threshold(wave, shrink):
    vmem = pl.BlockSpec(memory_space=pltpu.VMEM)
    return pl.pallas_call(
        threshold_kernel,
        out_shape=jax.ShapeDtypeStruct((ROWS, 128), jnp.float32),
        in_specs=[vmem, vmem],
        out_specs=pl.BlockSpec(memory_space=pl.ANY),
        scratch_shapes=[
            pltpu.VMEM((ROWS, 128), jnp.float32),
            pltpu.SemaphoreType.DMA((CHUNKS,)),
        ],
        compiler_params=pltpu.CompilerParams(vmem_limit_bytes=24 * 2**20),
        name="threshold",
    )(wave, shrink)


def body(traces, rates, byte_target):
    width = traces.shape[3]
    rows = traces.reshape(ROWS, width)
    wave, shrink = transform(rows, rates.reshape(PLANES, SHOTS), byte_target)
    return threshold(wave, shrink).reshape(SHOTS, 16, 4, width)


def solution(mesh):
    return jax.shard_map(
        body,
        mesh=mesh,
        in_specs=(P("line", None, None, "tm"), P("line", "tm", None, None), P()),
        out_specs=P(None, "line", None, "tm"),
        check_vma=False,
    )
```
